256 devices in a mesh: expert: 128 (over x, y, z), dp: 2 (over core).
Axes of the slice: x: 4, y: 4, z: 8, core: 2. Of those that a mesh axis runs over, the one named last changes fastest.
Arguments:
- tokens: bfloat16 [16384, 1024], P('expert'), may hold values from -6 to 6
- router_weight: bfloat16 [1024, 64], replicated, may hold values from -0.375 to 0.375
- gate_weight: bfloat16 [128, 1024, 2048], P('expert', None, 'dp'), may hold values from -0.1875 to 0.1875
- up_weight: bfloat16 [128, 1024, 2048], P('expert', None, 'dp'), may hold values from -0.1875 to 0.1875
- down_weight: bfloat16 [128, 2048, 1024], P('expert', 'dp'), may hold values from -0.1875 to 0.1875
- expand_weight: bfloat16 [1024, 8192], P(None, ('expert', 'dp')), may hold values from -0.5 to 0.5
- expert_ids: int32 [16384, 2], P('expert'), may hold values from 0 to 63, all different within a row; in each aligned block of 128 rows (0 to 127, 128 to 255, ...) at most 8 rows name the same one
- frame_slot: int32 [1024], P('expert'), may hold values from 0 to 1023, each once
Outputs:
- mixed: bfloat16 [16384, 1024], P('expert', 'dp')
- covariance: float32 [8192, 8192], P(('expert', 'dp'))
The draws below stay inside these ranges and needn't reach their ends.
Inputs may be any that keep to these rules, and one draw needn't show every extreme that they name: `expert_ids`: each row names 2 different experts; the rows of one device name each expert at most 8 times, and in every draw some device names some expert exactly 8 times. `frame_slot`: each number once.
All inputs are finite; a program needn't handle non-finite values.
Results may differ from the reference program's by a relative error of at most 0.02.
Values may be sent and summed in bfloat16 or wider, within the bound.
No kernel may reach another device: no remote copies, remote signals or barrier semaphores. Data moves between devices by JAX's collectives and lax.ppermute only.
A program may use at most 192 MiB of HBM per device.

```python
import math
import jax
import jax.numpy as jnp
import numpy as np
from jax import lax

D = 1024
FF = 4096
E2 = 8192
TOP = 2
CLIP_FR = 4
TOK_DEV = 128
EXPERTS = 64
CAP = 8
FR_TOK = 16
TOKENS = 16384
FRAMES = 1024
CLIPS = 256
N_EXPERT = 128


def levels(own_key, dims, cuts, least, high):
    def one(axis_at, blocks):
        heights = jax.random.uniform(jax.random.fold_in(jax.random.fold_in(own_key, 6), axis_at), (blocks,), jnp.float32, least / len(cuts), high / len(cuts))
        return jnp.repeat(jnp.exp(heights), dims[axis_at] // blocks).reshape((-1,) + (1,) * (len(dims) - axis_at - 1))

    level = one(*cuts[0])
    for cut in cuts[1:]:
        level = level * one(*cut)
    return level


def routed_block(own_key, own, number, rows, number_of, top, reach, slope):
    sequence = jax.random.permutation(own_key, number_of)
    crowded, common = shares(number_of, rows * top, reach, slope, True), shares(number_of, rows * top, reach, slope, False)
    places = jnp.arange(number_of)

    def named(sizes, turn):
        used = int((sizes > 0).sum())
        fixed = max(1, used // 4)
        shifted = fixed + (places - fixed + turn * (used - fixed)) % max(1, number_of - fixed)
        return jnp.zeros((number_of,), jnp.int32).at[sequence[jnp.where(places < fixed, places, shifted)]].set(jnp.asarray(sizes, jnp.int32))

    sizes = jnp.where(number % 4 == 0, named(crowded, number // 4), named(common, number - number // 4 - 1))
    mixed = jax.random.permutation(jax.random.fold_in(own, 3), number_of)
    giver, receiver = mixed[0:number_of // 2 * 2:2], mixed[1:number_of // 2 * 2:2]
    margin = jnp.minimum(sizes[giver] - 1, reach - sizes[receiver]) // 2
    margin = jnp.where((giver == sequence[0]) | (receiver == sequence[0]) | (sizes[receiver] == 0), 0, jnp.maximum(margin, 0))
    shifted = jax.random.randint(jax.random.fold_in(own, 4), (number_of // 2,), 0, 1 << 20) % (margin + 1)
    sizes = sizes.at[giver].add(-shifted).at[receiver].add(shifted)
    labels = jnp.searchsorted(jnp.cumsum(sizes), jnp.arange(rows * top), side="right").astype(jnp.int32)
    table = labels.reshape(top, rows).T
    table = table[jax.random.permutation(jax.random.fold_in(own, 1), rows)]
    turn = jax.random.randint(jax.random.fold_in(own, 2), (rows, 1), 0, top)
    return jnp.take_along_axis(table, (jnp.arange(top)[None, :] + turn) % top, axis=1)


def shares(amount, total, most, slope, full):
    portions = [(1 << 20) // math.isqrt(standing ** slope) + 1 for standing in range(1, amount + 1)]
    largest = most if full else min(most, max(-(-total // amount), total * portions[0] // sum(portions)))
    least = 1 if total - largest >= amount - 1 else 0
    holding, spare = [largest] + [least] * (amount - 1), total - largest - least * (amount - 1)
    while spare > 0:
        movable = [i for i in range(1, amount) if holding[i] < largest] or [i for i in range(1, amount) if holding[i] < most]
        mass, remaining = sum([portions[i] for i in movable]), spare
        for i in movable:
            addition = min(most - holding[i], max(1, remaining * portions[i] // mass), spare)
            holding[i] = holding[i] + addition
            spare = spare - addition
    return np.array(holding)


def centred(stream_key, shape, deviation, bound, cuts=(), kind=jnp.bfloat16):
    values = deviation * jax.random.normal(stream_key, shape, jnp.float32)
    if cuts:
        values = values * levels(stream_key, shape, cuts, -0.22, 0.18)
    return jnp.clip(values, -bound, bound).astype(kind)


def setup_inputs(seed: int = 0) -> dict:
    arg_keys = jax.random.split(jax.random.key(seed), 9)
    tokens = centred(arg_keys[0], (TOKENS, D), 1.0, 6.0, ((0, 128),))
    router_weight = centred(arg_keys[1], (D, EXPERTS), (D / 4) ** -0.5, 0.375)
    gate_weight = centred(arg_keys[2], (2 * EXPERTS, D, FF // 2), D ** -0.5, 0.1875, ((0, 128), (2, 2)))
    up_weight = centred(arg_keys[3], (2 * EXPERTS, D, FF // 2), D ** -0.5, 0.1875, ((0, 128), (2, 2)))
    down_weight = centred(arg_keys[4], (2 * EXPERTS, FF // 2, D), (FF / 4) ** -0.5, 0.1875, ((0, 128), (1, 2)))
    expand_weight = centred(arg_keys[5], (D, E2), (D / 8) ** -0.5, 0.5, ((1, 256),))
    expert_ids_keys = jax.random.split(jax.random.fold_in(arg_keys[6], 1), TOKENS // TOK_DEV)
    expert_ids_turns = jax.random.permutation(jax.random.fold_in(arg_keys[6], 3), TOKENS // TOK_DEV)
    expert_ids = jax.vmap(lambda own, number: routed_block(jax.random.fold_in(arg_keys[6], 2), own, number, TOK_DEV, EXPERTS, TOP, CAP, 2))(expert_ids_keys, expert_ids_turns).reshape((TOKENS, TOP))
    frame_slot = jax.random.permutation(arg_keys[7], FRAMES).astype(jnp.int32)
    return {"tokens": tokens, "router_weight": router_weight, "gate_weight": gate_weight, "up_weight": up_weight, "down_weight": down_weight, "expand_weight": expand_weight, "expert_ids": expert_ids, "frame_slot": frame_slot}


def reference(tokens, router_weight, gate_weight, up_weight, down_weight, expand_weight, expert_ids, frame_slot):
    logits = jnp.dot(tokens, router_weight, preferred_element_type=jnp.float32)
    hot = expert_ids[:, :, None] == jnp.arange(EXPERTS, dtype=jnp.int32)[None, None, :]
    chosen = jnp.sum(jnp.where(hot, logits[:, None, :], jnp.float32(0.0)), axis=-1)
    gates = jax.nn.sigmoid(chosen - chosen[:, ::-1])
    per_block = hot.astype(jnp.int32).reshape(N_EXPERT, TOK_DEV * TOP, EXPERTS)
    slot = jnp.sum((jnp.cumsum(per_block, axis=1) - per_block) * per_block, axis=-1)
    source = jnp.arange(N_EXPERT, dtype=jnp.int32)[:, None]
    routed = expert_ids.reshape(N_EXPERT, TOK_DEV * TOP)
    dest = (routed * (N_EXPERT * CAP) + source * CAP + slot).reshape(-1).astype(jnp.int32)
    repeated = jnp.repeat(tokens, TOP, axis=0)
    buffer = jnp.zeros((EXPERTS * N_EXPERT * CAP, D), jnp.bfloat16).at[dest].set(repeated)
    buffer = buffer.reshape(EXPERTS, N_EXPERT * CAP, D)
    quarter = FF // 4
    gates_w = gate_weight.reshape(EXPERTS, 2, D, FF // 2)
    ups_w = up_weight.reshape(EXPERTS, 2, D, FF // 2)
    downs_w = down_weight.reshape(EXPERTS, 2, FF // 2, D)

    def one_expert(operands):
        inputs, w_gate, w_up, w_down = operands
        total = jnp.zeros((N_EXPERT * CAP, D), jnp.float32)
        for half in range(2):
            for inner in range(2):
                lo = inner * quarter
                gate = jnp.dot(inputs, w_gate[half][:, lo:lo + quarter], preferred_element_type=jnp.float32)
                upper = jnp.dot(inputs, w_up[half][:, lo:lo + quarter], preferred_element_type=jnp.float32)
                hidden = (jax.nn.silu(gate) * upper).astype(jnp.bfloat16)
                piece = jnp.dot(hidden, w_down[half][lo:lo + quarter, :], preferred_element_type=jnp.float32).astype(jnp.bfloat16)
                piece = lax.optimization_barrier(piece)
                total = total + piece.astype(jnp.float32)
        return total

    outputs = lax.map(one_expert, (buffer, gates_w, ups_w, downs_w))
    picked = outputs.reshape(EXPERTS * N_EXPERT * CAP, D)[dest].reshape(TOKENS, TOP, D)
    moe = jnp.sum(picked * gates[:, :, None], axis=1)
    mixed = (tokens.astype(jnp.float32) + moe).astype(jnp.bfloat16)
    frames = jnp.mean(mixed.reshape(FRAMES, FR_TOK, D), axis=1, dtype=jnp.float32).astype(jnp.bfloat16)
    packed = jnp.zeros((FRAMES, D), jnp.bfloat16).at[frame_slot].set(frames)
    clips = jnp.mean(packed.reshape(CLIPS, CLIP_FR, D), axis=1, dtype=jnp.float32).astype(jnp.bfloat16)
    embed = jnp.dot(clips, expand_weight, preferred_element_type=jnp.float32)
    centered = embed - jnp.mean(embed, axis=0, keepdims=True)
    covariance = jnp.dot(centered.T, centered, precision=lax.Precision.HIGHEST, preferred_element_type=jnp.float32) / (CLIPS - 1)
    return mixed, covariance
```

```python
import functools

import jax
import jax.numpy as jnp
from jax import lax
from jax.experimental import pallas as pl
from jax.experimental.pallas import tpu as pltpu
from jax.sharding import Mesh, PartitionSpec as P

EXP = ("x", "y", "z")
ALL = ("x", "y", "z", "dp")
F32 = jnp.float32
BF16 = jnp.bfloat16
LANES = 128
NT = (((1,), (1,)), ((), ()))
TN = (((0,), (0,)), ((), ()))


def dot(a, b):
    return jnp.dot(a, b, preferred_element_type=F32)


def dot_nt(a, b):
    return lax.dot_general(a, b, NT, preferred_element_type=F32)


def dot_tn(a, b):
    return lax.dot_general(a, b, TN, preferred_element_type=F32)


def split2(v):
    high = v.astype(BF16)
    return high, (v - high.astype(F32)).astype(BF16)


def half(start, size):
    return pl.ds(pl.multiple_of(start * size, LANES), size)


def prep_kernel(capacity, d_ref, tok_ref, router_ref, ids_ref, out_ref, high_ref, low_ref):
    d = d_ref[0]
    rows, width = tok_ref.shape
    experts = router_ref.shape[0]
    logits = dot_nt(router_ref[...], tok_ref[...])
    number = lax.broadcasted_iota(jnp.int32, (experts, rows), 0)
    hot0 = ids_ref[0:1, :] == number
    hot1 = ids_ref[1:2, :] == number
    chosen0 = jnp.sum(jnp.where(hot0, logits, 0.0), axis=0, keepdims=True)
    chosen1 = jnp.sum(jnp.where(hot1, logits, 0.0), axis=0, keepdims=True)
    gate = jnp.where(hot0, jax.nn.sigmoid(chosen0 - chosen1), 0.0) + jnp.where(
        hot1, jax.nn.sigmoid(chosen1 - chosen0), 0.0
    )
    member = jnp.where(hot0 | hot1, 1.0, 0.0)
    before = lax.broadcasted_iota(jnp.int32, (rows, rows), 0) < lax.broadcasted_iota(
        jnp.int32, (rows, rows), 1
    )
    earlier = dot(member.astype(BF16), jnp.where(before, 1.0, 0.0).astype(BF16))
    place = jnp.where(member > 0.0, earlier, -1.0)
    slots = lax.broadcasted_iota(jnp.int32, (experts, 2, capacity, rows), 2).astype(F32)
    taken = place[:, None, None, :] == slots
    picks = jnp.where(taken, 1.0, 0.0).reshape(experts * 2 * capacity, rows)
    weights = jnp.where(taken, gate[:, None, None, :], 0.0).reshape(experts * 2 * capacity, rows)
    high, low = split2(weights)
    high_ref[...] = high
    low_ref[...] = low
    out_ref[...] = dot(picks.astype(BF16), tok_ref[:, half(d, width // 2)]).astype(BF16)


def ffn_kernel(
    step_rows, d_ref, own_ref, other_ref, gate_ref, up_ref, down_hbm, out_ref, down_ref, hid_ref, sem
):
    d = d_ref[0]
    j = pl.program_id(0)
    steps = pl.num_programs(0)
    rows, part = own_ref.shape
    copy = pltpu.make_async_copy(down_hbm, down_ref, sem)

    @pl.when(j == 0)
    def _():
        copy.start()

    def hidden(m, carry):
        at = pl.ds(pl.multiple_of(m * step_rows, step_rows), step_rows)
        own, other = own_ref[at, :], other_ref[at, :]
        mine, theirs = half(d, part), half(1 - d, part)
        gate = dot(own, gate_ref[mine, :]) + dot(other, gate_ref[theirs, :])
        upper = dot(own, up_ref[mine, :]) + dot(other, up_ref[theirs, :])
        hid_ref[j, at, :] = (gate * jax.nn.sigmoid(gate) * upper).astype(BF16)
        return carry

    lax.fori_loop(0, rows // step_rows, hidden, 0)

    @pl.when(j == steps - 1)
    def _():
        copy.wait()
        block = hid_ref.shape[2]

        def down(m, carry):
            at = pl.ds(pl.multiple_of(m * step_rows, step_rows), step_rows)
            for which, cols in enumerate((half(1 - d, part), half(d, part))):
                total = dot(hid_ref[0, at, :], down_ref[0:block, cols])
                for s in range(1, hid_ref.shape[0]):
                    total = total + dot(hid_ref[s, at, :], down_ref[s * block : (s + 1) * block, cols])
                out_ref[which, at, :] = total.astype(BF16)
            return carry

        lax.fori_loop(0, rows // step_rows, down, 0)


def combine_kernel(d_ref, back_ref, high_ref, low_ref, tok_ref, slot_ref, mixed_ref, frames_ref):
    d = d_ref[0]
    rows, part = mixed_ref.shape
    count = slot_ref.shape[0]
    back = back_ref[...]
    moe = dot_tn(high_ref[...], back) + dot_tn(low_ref[...], back)
    mixed = (tok_ref[:, half(d, part)].astype(F32) + moe).astype(BF16)
    mixed_ref[...] = mixed
    length = rows // count
    frames = jnp.sum(mixed.astype(F32).reshape(count, length, part), axis=1) / length
    frames_ref[:, 0:part] = frames.astype(BF16)
    slot = slot_ref[...]
    lane = lax.broadcasted_iota(jnp.int32, (count, LANES), 1)
    digits = jnp.where(lane == 0, slot // 32, jnp.where(lane == 1, slot % 32, 0))
    frames_ref[:, part : part + LANES] = digits.astype(F32).astype(BF16)


def clip_kernel(length, frames_ref, digits_ref, clips_ref):
    clips, part = clips_ref.shape
    count = frames_ref.shape[0]
    digits = digits_ref[...].astype(F32)
    slot = digits[0:1, :] * 32.0 + digits[1:2, :]
    clip = jnp.floor(slot / length)
    number = lax.broadcasted_iota(jnp.int32, (clips, count), 0).astype(F32)
    picks = jnp.where(clip == number, 1.0, 0.0).astype(BF16)
    clips_ref[...] = (dot(picks, frames_ref[:, 0:part]) / length).astype(BF16)


def cov_kernel(d_ref, own_ref, other_ref, mine_ref, full_ref, out_ref, left_ref):
    d = d_ref[0]
    cols = mine_ref.shape[0]
    clips, part = own_ref.shape

    @pl.when(pl.program_id(0) == 0)
    def _():
        own, other = own_ref[...], other_ref[...]
        embed = dot_nt(mine_ref[:, half(d, part)], own) + dot_nt(mine_ref[:, half(1 - d, part)], other)
        centered = embed - jnp.mean(embed, axis=1, keepdims=True)
        high = centered.astype(BF16)
        rest = centered - high.astype(F32)
        middle = rest.astype(BF16)
        low = (rest - middle.astype(F32)).astype(BF16)
        for where, clip in ((half(d, part), own), (half(1 - d, part), other)):
            left = (dot(high, clip) + dot(middle, clip) + dot(low, clip)) / (clips - 1)
            left_high, left_low = split2(left)
            left_ref[0:cols, where] = left_high
            left_ref[cols : 2 * cols, where] = left_low

    both = dot_nt(left_ref[...], full_ref[...])
    out_ref[...] = both[0:cols] + both[cols : 2 * cols]


SCALAR = pl.BlockSpec(memory_space=pltpu.SMEM)


def per_device(
    tokens,
    router_weight,
    gate_weight,
    up_weight,
    down_weight,
    expand_weight,
    expert_ids,
    frame_slot,
):
    tok_rows, width = tokens.shape
    experts = router_weight.shape[1]
    n_expert = lax.axis_size(EXP)
    n_z = lax.axis_size("z")
    n_xy = n_expert // n_z
    capacity = 4 * tok_rows // experts
    part = width // 2
    hidden = gate_weight.shape[2]
    rows = n_expert * capacity
    count = frame_slot.shape[0]
    frame_total = count * n_expert
    clip_total = frame_total // 4
    share = expand_weight.shape[1]
    d = lax.axis_index("dp").astype(jnp.int32).reshape(1)
    swap = [(0, 1), (1, 0)]
    params = pltpu.CompilerParams(vmem_limit_bytes=48 * 2**20)

    mine = expand_weight.T
    full = lax.all_gather(mine, ALL, axis=0, tiled=True)

    vmem = pl.BlockSpec(memory_space=pltpu.VMEM)
    outgoing, high, low = pl.pallas_call(
        functools.partial(prep_kernel, capacity),
        out_shape=(
            jax.ShapeDtypeStruct((rows, part), BF16),
            jax.ShapeDtypeStruct((rows, tok_rows), BF16),
            jax.ShapeDtypeStruct((rows, tok_rows), BF16),
        ),
        in_specs=[SCALAR, vmem, vmem, vmem],
        out_specs=(vmem, vmem, vmem),
        compiler_params=params,
        name="prep",
    )(d, tokens, router_weight.T, expert_ids.T)

    received = lax.all_to_all(
        outgoing.reshape(n_expert, capacity, part), EXP, split_axis=0, concat_axis=0, tiled=True
    ).reshape(rows, part)
    other = lax.ppermute(received, "dp", swap)

    block = min(256, hidden)
    pieces = pl.pallas_call(
        functools.partial(ffn_kernel, 256),
        out_shape=jax.ShapeDtypeStruct((2, rows, part), BF16),
        grid=(hidden // block,),
        in_specs=[
            SCALAR,
            pl.BlockSpec((rows, part), lambda j: (0, 0)),
            pl.BlockSpec((rows, part), lambda j: (0, 0)),
            pl.BlockSpec((None, width, block), lambda j: (0, 0, j)),
            pl.BlockSpec((None, width, block), lambda j: (0, 0, j)),
            pl.BlockSpec(memory_space=pl.ANY),
        ],
        out_specs=pl.BlockSpec((2, rows, part), lambda j: (0, 0, 0)),
        scratch_shapes=[
            pltpu.VMEM((hidden, width), BF16),
            pltpu.VMEM((hidden // block, rows, block), BF16),
            pltpu.SemaphoreType.DMA(()),
        ],
        compiler_params=params,
        name="ffn",
    )(d, received, other, gate_weight, up_weight, down_weight.reshape(hidden, width))

    brought = lax.ppermute(pieces[0], "dp", swap)
    summed = (pieces[1].astype(F32) + brought.astype(F32)).astype(BF16)
    back = lax.all_to_all(
        summed.reshape(n_expert, capacity, part), EXP, split_axis=0, concat_axis=0, tiled=True
    ).reshape(rows, part)

    mixed, frames = pl.pallas_call(
        combine_kernel,
        out_shape=(
            jax.ShapeDtypeStruct((tok_rows, part), BF16),
            jax.ShapeDtypeStruct((count, part + LANES), BF16),
        ),
        in_specs=[SCALAR, vmem, vmem, vmem, vmem, vmem],
        out_specs=(vmem, vmem),
        compiler_params=params,
        name="combine",
    )(d, back, high, low, tokens, frame_slot.reshape(count, 1))

    def spread(block, axes, size):
        copies = jnp.broadcast_to(block[None], (size,) + block.shape)
        out = lax.all_to_all(copies, axes, split_axis=0, concat_axis=0, tiled=True)
        return out.reshape(-1, block.shape[-1])

    gathered = spread(spread(frames, "z", n_z), ("x", "y"), n_xy)
    digits = gathered[:, part : part + 8].T
    clips = pl.pallas_call(
        functools.partial(clip_kernel, 4),
        out_shape=jax.ShapeDtypeStruct((clip_total, part), BF16),
        in_specs=[vmem, vmem],
        out_specs=vmem,
        compiler_params=params,
        name="clips",
    )(gathered, digits)
    other_clips = lax.ppermute(clips, "dp", swap)

    total_cols = full.shape[0]
    wide = 1024
    whole = lambda shape: pl.BlockSpec(shape, lambda j: (0,) * len(shape))
    covariance = pl.pallas_call(
        cov_kernel,
        out_shape=jax.ShapeDtypeStruct((share, total_cols), F32),
        grid=(total_cols // wide,),
        in_specs=[
            SCALAR,
            whole((clip_total, part)),
            whole((clip_total, part)),
            whole((share, width)),
            pl.BlockSpec((wide, width), lambda j: (j, 0)),
        ],
        out_specs=pl.BlockSpec((share, wide), lambda j: (0, j)),
        scratch_shapes=[pltpu.VMEM((2 * share, width), BF16)],
        compiler_params=params,
        name="covariance",
    )(d, clips, other_clips, mine, full)
    return mixed, covariance


def solution(mesh):
    grid = Mesh(mesh.devices.reshape(4, 4, 8, 2), ALL)
    return jax.shard_map(
        per_device,
        mesh=grid,
        in_specs=(
            P(EXP, None),
            P(),
            P(EXP, None, "dp"),
            P(EXP, None, "dp"),
            P(EXP, "dp", None),
            P(None, ALL),
            P(EXP, None),
            P(EXP),
        ),
        out_specs=(P(EXP, "dp"), P(ALL, None)),
        check_vma=False,
    )
```

```python
import functools

import jax
import jax.numpy as jnp
from jax import lax
from jax.experimental import pallas as pl
from jax.experimental.pallas import tpu as pltpu
from jax.sharding import Mesh, PartitionSpec as P

EXP = ("x", "y", "z")
ALL = ("x", "y", "z", "dp")
F32 = jnp.float32
BF16 = jnp.bfloat16
LANES = 128
NT = (((1,), (1,)), ((), ()))
TN = (((0,), (0,)), ((), ()))


def dot(a, b):
    return jnp.dot(a, b, preferred_element_type=F32)


def dot_nt(a, b):
    return lax.dot_general(a, b, NT, preferred_element_type=F32)


def dot_tn(a, b):
    return lax.dot_general(a, b, TN, preferred_element_type=F32)


def split2(v):
    high = v.astype(BF16)
    return high, (v - high.astype(F32)).astype(BF16)


def half(start, size):
    return pl.ds(pl.multiple_of(start * size, LANES), size)


def prep_kernel(
    capacity, d_ref, tok_hbm, router_hbm, ids_hbm, out_ref, high_ref, low_ref, tok_ref, router_ref, ids_ref, sems
):
    copies = [
        pltpu.make_async_copy(source, target, sems.at[k])
        for k, (source, target) in enumerate(
            ((tok_hbm, tok_ref), (router_hbm, router_ref), (ids_hbm, ids_ref))
        )
    ]
    for copy in copies:
        copy.start()
    for copy in copies:
        copy.wait()
    d = d_ref[0]
    rows, width = tok_ref.shape
    experts = router_ref.shape[0]
    logits = dot_nt(router_ref[...], tok_ref[...])
    number = lax.broadcasted_iota(jnp.int32, (experts, rows), 0)
    hot0 = ids_ref[0:1, :] == number
    hot1 = ids_ref[1:2, :] == number
    chosen0 = jnp.sum(jnp.where(hot0, logits, 0.0), axis=0, keepdims=True)
    chosen1 = jnp.sum(jnp.where(hot1, logits, 0.0), axis=0, keepdims=True)
    gate = jnp.where(hot0, jax.nn.sigmoid(chosen0 - chosen1), 0.0) + jnp.where(
        hot1, jax.nn.sigmoid(chosen1 - chosen0), 0.0
    )
    member = jnp.where(hot0 | hot1, 1.0, 0.0)
    before = lax.broadcasted_iota(jnp.int32, (rows, rows), 0) < lax.broadcasted_iota(
        jnp.int32, (rows, rows), 1
    )
    earlier = dot(member.astype(BF16), jnp.where(before, 1.0, 0.0).astype(BF16))
    place = jnp.where(member > 0.0, earlier, -1.0)
    slots = lax.broadcasted_iota(jnp.int32, (experts, 2, capacity, rows), 2).astype(F32)
    taken = place[:, None, None, :] == slots
    picks = jnp.where(taken, 1.0, 0.0).reshape(experts * 2 * capacity, rows)
    weights = jnp.where(taken, gate[:, None, None, :], 0.0).reshape(experts * 2 * capacity, rows)
    high, low = split2(weights)
    high_ref[...] = high
    low_ref[...] = low
    out_ref[...] = dot(picks.astype(BF16), tok_ref[:, half(d, width // 2)]).astype(BF16)


def ffn_kernel(
    step, d_ref, own_ref, other_ref, gate_hbm, up_hbm, down_hbm, hid_ref, out_ref, x_ref, gate_ref, up_ref, down_ref, sems, down_sem
):
    d = d_ref[0]
    rows, part = own_ref.shape
    blocks = sems.shape[1]
    block = gate_ref.shape[1] // blocks
    spans = [slice(k * block, (k + 1) * block) for k in range(blocks)]
    loads = [
        [
            pltpu.make_async_copy(source.at[:, span], target.at[:, span], sems.at[w, k])
            for w, (source, target) in enumerate(((gate_hbm, gate_ref), (up_hbm, up_ref)))
        ]
        for k, span in enumerate(spans)
    ]
    load_down = pltpu.make_async_copy(down_hbm, down_ref, down_sem)
    for pair in loads:
        for load in pair:
            load.start()
    load_down.start()
    x_ref[:, half(d, part)] = own_ref[...]
    x_ref[:, half(1 - d, part)] = other_ref[...]

    for pair, span in zip(loads, spans):
        for load in pair:
            load.wait()

        def body(m, carry, span=span):
            at = pl.ds(pl.multiple_of(m * step, step), step)
            gate = dot(x_ref[at, :], gate_ref[:, span])
            upper = dot(x_ref[at, :], up_ref[:, span])
            hid_ref[at, span] = (gate * jax.nn.sigmoid(gate) * upper).astype(BF16)
            return carry

        lax.fori_loop(0, rows // step, body, 0)

    load_down.wait()

    def last(m, carry):
        at = pl.ds(pl.multiple_of(m * step, step), step)
        out_ref[at, :] = dot(hid_ref[at, :], down_ref[:, half(1 - d, part)]).astype(BF16)
        return carry

    lax.fori_loop(0, rows // step, last, 0)


def own_kernel(d_ref, hid_ref, down_ref, out_ref):
    out_ref[...] = dot(hid_ref[...], down_ref[:, half(d_ref[0], out_ref.shape[1])])


def add_kernel(own_ref, brought_ref, out_ref):
    out_ref[...] = (own_ref[...] + brought_ref[...].astype(F32)).astype(BF16)


def combine_kernel(d_ref, back_ref, high_ref, low_ref, tok_ref, slot_ref, mixed_ref, frames_ref):
    d = d_ref[0]
    rows, part = mixed_ref.shape
    count = slot_ref.shape[0]
    back = back_ref[...]
    moe = dot_tn(high_ref[...], back) + dot_tn(low_ref[...], back)
    mixed = (tok_ref[:, half(d, part)].astype(F32) + moe).astype(BF16)
    mixed_ref[...] = mixed
    length = rows // count
    frames = jnp.sum(mixed.astype(F32).reshape(count, length, part), axis=1) / length
    frames_ref[:, 0:part] = frames.astype(BF16)
    slot = slot_ref[...]
    lane = lax.broadcasted_iota(jnp.int32, (count, LANES), 1)
    digits = jnp.where(lane == 0, slot // 32, jnp.where(lane == 1, slot % 32, 0))
    frames_ref[:, part : part + LANES] = digits.astype(F32).astype(BF16)


def clip_kernel(length, frames_ref, digits_ref, clips_ref):
    clips, part = clips_ref.shape
    count = frames_ref.shape[0]
    digits = digits_ref[...].astype(F32)
    slot = digits[0:1, :] * 32.0 + digits[1:2, :]
    clip = jnp.floor(slot / length)
    number = lax.broadcasted_iota(jnp.int32, (clips, count), 0).astype(F32)
    picks = jnp.where(clip == number, 1.0, 0.0).astype(BF16)
    clips_ref[...] = (dot(picks, frames_ref[:, 0:part]) / length).astype(BF16)


def cov_kernel(
    d_ref, own_ref, other_ref, mine_ref, full_hbm, out_hbm, left_ref, full_ref, out_ref, in_sems, out_sems
):
    d = d_ref[0]
    cols = mine_ref.shape[0]
    clips, part = own_ref.shape
    blocks = in_sems.shape[0]
    wide = full_ref.shape[0] // blocks
    spans = [slice(k * wide, (k + 1) * wide) for k in range(blocks)]
    loads = [
        pltpu.make_async_copy(full_hbm.at[span, :], full_ref.at[span, :], in_sems.at[k])
        for k, span in enumerate(spans)
    ]
    stores = [
        pltpu.make_async_copy(out_ref.at[:, span], out_hbm.at[:, span], out_sems.at[k])
        for k, span in enumerate(spans)
    ]
    for load in loads:
        load.start()
    own, other = own_ref[...], other_ref[...]
    embed = dot_nt(mine_ref[:, half(d, part)], own) + dot_nt(mine_ref[:, half(1 - d, part)], other)
    centered = embed - jnp.mean(embed, axis=1, keepdims=True)
    high = centered.astype(BF16)
    rest = centered - high.astype(F32)
    middle = rest.astype(BF16)
    low = (rest - middle.astype(F32)).astype(BF16)
    for where, clip in ((half(d, part), own), (half(1 - d, part), other)):
        left = (dot(high, clip) + dot(middle, clip) + dot(low, clip)) / (clips - 1)
        left_high, left_low = split2(left)
        left_ref[0:cols, where] = left_high
        left_ref[cols : 2 * cols, where] = left_low
    for load, store, span in zip(loads, stores, spans):
        load.wait()
        both = dot_nt(left_ref[...], full_ref[span, :])
        out_ref[:, span] = both[0:cols] + both[cols : 2 * cols]
        store.start()
    for store in stores:
        store.wait()


SCALAR = pl.BlockSpec(memory_space=pltpu.SMEM)


def per_device(
    tokens,
    router_weight,
    gate_weight,
    up_weight,
    down_weight,
    expand_weight,
    expert_ids,
    frame_slot,
):
    tok_rows, width = tokens.shape
    experts = router_weight.shape[1]
    n_expert = lax.axis_size(EXP)
    n_z = lax.axis_size("z")
    n_xy = n_expert // n_z
    capacity = 4 * tok_rows // experts
    part = width // 2
    hidden = gate_weight.shape[2]
    rows = n_expert * capacity
    count = frame_slot.shape[0]
    frame_total = count * n_expert
    clip_total = frame_total // 4
    share = expand_weight.shape[1]
    d = lax.axis_index("dp").astype(jnp.int32).reshape(1)
    swap = [(0, 1), (1, 0)]
    params = pltpu.CompilerParams(vmem_limit_bytes=16 * 2**20)

    mine = expand_weight.T
    full = lax.all_gather(mine, ALL, axis=0, tiled=True)

    vmem = pl.BlockSpec(memory_space=pltpu.VMEM)
    hbm = pl.BlockSpec(memory_space=pl.ANY)
    outgoing, high, low = pl.pallas_call(
        functools.partial(prep_kernel, capacity),
        out_shape=(
            jax.ShapeDtypeStruct((rows, part), BF16),
            jax.ShapeDtypeStruct((rows, tok_rows), BF16),
            jax.ShapeDtypeStruct((rows, tok_rows), BF16),
        ),
        in_specs=[SCALAR, hbm, hbm, hbm],
        out_specs=(vmem, vmem, vmem),
        scratch_shapes=[
            pltpu.VMEM(tokens.shape, BF16),
            pltpu.VMEM((experts, width), BF16),
            pltpu.VMEM((2, tok_rows), jnp.int32),
            pltpu.SemaphoreType.DMA((3,)),
        ],
        compiler_params=pltpu.CompilerParams(vmem_limit_bytes=57 * 2**20),
        name="prep",
    )(d, tokens, router_weight.T, expert_ids.T)

    received = lax.all_to_all(
        outgoing.reshape(n_expert, capacity, part), EXP, split_axis=0, concat_axis=0, tiled=True
    ).reshape(rows, part)
    other = lax.ppermute(received, "dp", swap)

    w_down = down_weight.reshape(hidden, width)
    inner, theirs = pl.pallas_call(
        functools.partial(ffn_kernel, 512),
        out_shape=(
            jax.ShapeDtypeStruct((rows, hidden), BF16),
            jax.ShapeDtypeStruct((rows, part), BF16),
        ),
        in_specs=[SCALAR, vmem, vmem, hbm, hbm, hbm],
        out_specs=(vmem, vmem),
        scratch_shapes=[
            pltpu.VMEM((rows, width), BF16),
            pltpu.VMEM((width, hidden), BF16),
            pltpu.VMEM((width, hidden), BF16),
            pltpu.VMEM((hidden, width), BF16),
            pltpu.SemaphoreType.DMA((2, 4)),
            pltpu.SemaphoreType.DMA(()),
        ],
        compiler_params=pltpu.CompilerParams(vmem_limit_bytes=48 * 2**20),
        cost_estimate=pl.CostEstimate(
            flops=2 * rows * hidden * (2 * width + part), bytes_accessed=0, transcendentals=0
        ),
        name="ffn",
    )(d, received, other, gate_weight.reshape(width, hidden), up_weight.reshape(width, hidden), w_down)

    brought = lax.ppermute(theirs, "dp", swap)
    ours = pl.pallas_call(
        own_kernel,
        out_shape=jax.ShapeDtypeStruct((rows, part), F32),
        in_specs=[SCALAR, vmem, vmem],
        out_specs=vmem,
        compiler_params=params,
        cost_estimate=pl.CostEstimate(flops=2 * rows * hidden * part, bytes_accessed=0, transcendentals=0),
        name="ours",
    )(d, inner, w_down)
    summed = pl.pallas_call(
        add_kernel,
        out_shape=jax.ShapeDtypeStruct((rows, part), BF16),
        in_specs=[vmem, vmem],
        out_specs=vmem,
        compiler_params=params,
        name="total",
    )(ours, brought)
    back = lax.all_to_all(
        summed.reshape(n_expert, capacity, part), EXP, split_axis=0, concat_axis=0, tiled=True
    ).reshape(rows, part)

    mixed, frames = pl.pallas_call(
        combine_kernel,
        out_shape=(
            jax.ShapeDtypeStruct((tok_rows, part), BF16),
            jax.ShapeDtypeStruct((count, part + LANES), BF16),
        ),
        in_specs=[SCALAR, vmem, vmem, vmem, vmem, vmem],
        out_specs=(vmem, vmem),
        compiler_params=params,
        name="combine",
    )(d, back, high, low, tokens, frame_slot.reshape(count, 1))

    def spread(block, axes, size):
        copies = jnp.broadcast_to(block[None], (size,) + block.shape)
        out = lax.all_to_all(copies, axes, split_axis=0, concat_axis=0, tiled=True)
        return out.reshape(-1, block.shape[-1])

    gathered = spread(spread(frames, "z", n_z), ("x", "y"), n_xy)
    digits = gathered[:, part : part + 8].T
    clips = pl.pallas_call(
        functools.partial(clip_kernel, 4),
        out_shape=jax.ShapeDtypeStruct((clip_total, part), BF16),
        in_specs=[vmem, vmem],
        out_specs=vmem,
        compiler_params=params,
        name="clips",
    )(gathered, digits)
    other_clips = lax.ppermute(clips, "dp", swap)

    total_cols = full.shape[0]
    blocks = 8
    covariance = pl.pallas_call(
        cov_kernel,
        out_shape=jax.ShapeDtypeStruct((share, total_cols), F32),
        in_specs=[SCALAR, vmem, vmem, vmem, hbm],
        out_specs=hbm,
        scratch_shapes=[
            pltpu.VMEM((2 * share, width), BF16),
            pltpu.VMEM((total_cols, width), BF16),
            pltpu.VMEM((share, total_cols), F32),
            pltpu.SemaphoreType.DMA((blocks,)),
            pltpu.SemaphoreType.DMA((blocks,)),
        ],
        compiler_params=pltpu.CompilerParams(vmem_limit_bytes=48 * 2**20),
        name="covariance",
    )(d, clips, other_clips, mine, full)
    return mixed, covariance


def solution(mesh):
    grid = Mesh(mesh.devices.reshape(4, 4, 8, 2), ALL)
    return jax.shard_map(
        per_device,
        mesh=grid,
        in_specs=(
            P(EXP, None),
            P(),
            P(EXP, None, "dp"),
            P(EXP, None, "dp"),
            P(EXP, "dp", None),
            P(None, ALL),
            P(EXP, None),
            P(EXP),
        ),
        out_specs=(P(EXP, "dp"), P(ALL, None)),
        check_vma=False,
    )
```

```python
import functools

import jax
import jax.numpy as jnp
from jax import lax
from jax.experimental import pallas as pl
from jax.experimental.pallas import tpu as pltpu
from jax.sharding import Mesh, PartitionSpec as P

EXP = ("x", "y", "z")
ALL = ("x", "y", "z", "dp")
PLANE = ("x", "y")
F32 = jnp.float32
BF16 = jnp.bfloat16
LANES = 128
NT = (((1,), (1,)), ((), ()))
TN = (((0,), (0,)), ((), ()))


def dot(a, b):
    return jnp.dot(a, b, preferred_element_type=F32)


def dot_nt(a, b):
    return lax.dot_general(a, b, NT, preferred_element_type=F32)


def dot_tn(a, b):
    return lax.dot_general(a, b, TN, preferred_element_type=F32)


def split2(v):
    high = v.astype(BF16)
    return high, (v - high.astype(F32)).astype(BF16)


def half(start, size):
    return pl.ds(pl.multiple_of(start * size, LANES), size)


def prep_kernel(
    capacity, d_ref, tok_hbm, router_hbm, ids_hbm, out_ref, high_ref, low_ref, tok_ref, router_ref, ids_ref, sems
):
    copies = [
        pltpu.make_async_copy(source, target, sems.at[k])
        for k, (source, target) in enumerate(
            ((tok_hbm, tok_ref), (router_hbm, router_ref), (ids_hbm, ids_ref))
        )
    ]
    for copy in copies:
        copy.start()
    for copy in copies:
        copy.wait()
    d = d_ref[0]
    rows, width = tok_ref.shape
    experts = router_ref.shape[0]
    logits = dot_nt(router_ref[...], tok_ref[...])
    number = lax.broadcasted_iota(jnp.int32, (experts, rows), 0)
    hot0 = ids_ref[0:1, :] == number
    hot1 = ids_ref[1:2, :] == number
    chosen0 = jnp.sum(jnp.where(hot0, logits, 0.0), axis=0, keepdims=True)
    chosen1 = jnp.sum(jnp.where(hot1, logits, 0.0), axis=0, keepdims=True)
    gate = jnp.where(hot0, jax.nn.sigmoid(chosen0 - chosen1), 0.0) + jnp.where(
        hot1, jax.nn.sigmoid(chosen1 - chosen0), 0.0
    )
    member = jnp.where(hot0 | hot1, 1.0, 0.0)
    before = lax.broadcasted_iota(jnp.int32, (rows, rows), 0) < lax.broadcasted_iota(
        jnp.int32, (rows, rows), 1
    )
    earlier = dot(member.astype(BF16), jnp.where(before, 1.0, 0.0).astype(BF16))
    place = jnp.where(member > 0.0, earlier, -1.0)
    slots = lax.broadcasted_iota(jnp.int32, (experts, 2, capacity, rows), 2).astype(F32)
    taken = place[:, None, None, :] == slots
    picks = jnp.where(taken, 1.0, 0.0).reshape(experts * 2 * capacity, rows)
    weights = jnp.where(taken, gate[:, None, None, :], 0.0).reshape(experts * 2 * capacity, rows)
    high, low = split2(weights)
    high_ref[...] = high
    low_ref[...] = low
    out_ref[...] = dot(picks.astype(BF16), tok_ref[:, half(d, width // 2)]).astype(BF16)


def order_kernel(*refs):
    pass


def ffn_kernel(
    step, d_ref, own_ref, other_ref, gate_hbm, up_hbm, down_hbm, hid_ref, out_ref, x_ref, gate_ref, up_ref, down_ref, sems, down_sem
):
    d = d_ref[0]
    rows, part = own_ref.shape
    blocks = sems.shape[1]
    block = gate_ref.shape[1] // blocks
    spans = [slice(k * block, (k + 1) * block) for k in range(blocks)]
    loads = [
        [
            pltpu.make_async_copy(source.at[:, span], target.at[:, span], sems.at[w, k])
            for w, (source, target) in enumerate(((gate_hbm, gate_ref), (up_hbm, up_ref)))
        ]
        for k, span in enumerate(spans)
    ]
    load_down = pltpu.make_async_copy(down_hbm, down_ref, down_sem)
    for pair in loads:
        for load in pair:
            load.start()
    load_down.start()
    x_ref[:, half(d, part)] = own_ref[...]
    x_ref[:, half(1 - d, part)] = other_ref[...]

    for pair, span in zip(loads, spans):
        for load in pair:
            load.wait()

        def body(m, carry, span=span):
            at = pl.ds(pl.multiple_of(m * step, step), step)
            gate = dot(x_ref[at, :], gate_ref[:, span])
            upper = dot(x_ref[at, :], up_ref[:, span])
            hid_ref[at, span] = (gate * jax.nn.sigmoid(gate) * upper).astype(BF16)
            return carry

        lax.fori_loop(0, rows // step, body, 0)

    load_down.wait()

    def last(m, carry):
        at = pl.ds(pl.multiple_of(m * step, step), step)
        out_ref[at, :] = dot(hid_ref[at, :], down_ref[:, half(1 - d, part)]).astype(BF16)
        return carry

    lax.fori_loop(0, rows // step, last, 0)


def own_kernel(d_ref, hid_ref, down_ref, out_ref):
    out_ref[...] = dot(hid_ref[...], down_ref[:, half(d_ref[0], out_ref.shape[1])])


def add_kernel(own_ref, brought_ref, out_ref):
    out_ref[...] = (own_ref[...] + brought_ref[...].astype(F32)).astype(BF16)


def combine_kernel(d_ref, z_ref, back_ref, high_ref, low_ref, tok_ref, slot_ref, *refs):
    mixed_ref, payload_ref = refs[-2:]
    d, z = d_ref[0], z_ref[0]
    rows, part = mixed_ref.shape
    count = slot_ref.shape[0]
    back = back_ref[...]
    moe = dot_tn(high_ref[...], back) + dot_tn(low_ref[...], back)
    mixed = (tok_ref[:, half(d, part)].astype(F32) + moe).astype(BF16)
    mixed_ref[...] = mixed
    length = rows // count
    frames = jnp.sum(mixed.astype(F32).reshape(count, length, part), axis=1) / length
    slot = slot_ref[...]
    lane = lax.broadcasted_iota(jnp.int32, (count, part), 1)
    number = lax.broadcasted_iota(jnp.int32, (count, part), 0)
    digit = jnp.where(lane % (2 * count) < count, slot // 32, slot % 32)
    here = (lane // (2 * count) == z) & (lane % count == number)
    digits = jnp.sum(jnp.where(here, digit, 0).astype(F32), axis=0, keepdims=True)
    first = jnp.where(number == 0, jnp.broadcast_to(digits, (count, part)), 0.0)
    block = jnp.concatenate([frames, first], axis=0).astype(BF16)
    for k in range(payload_ref.shape[0]):
        payload_ref[k] = block


def clip_kernel(length, used, z_ref, frames_ref, digits_ref, *refs):
    line_refs, (clips_ref, embed_ref) = refs[:-2], refs[-2:]
    clips, part = clips_ref.shape
    groups = frames_ref.shape[0]
    digits = digits_ref[...].astype(F32)
    slot = digits[0:1, :] * 32.0 + digits[1:2, :]
    clip = jnp.floor(slot / length)
    number = lax.broadcasted_iota(jnp.int32, (clips, groups * used), 0).astype(F32)
    picks = jnp.where(clip == number, 1.0, 0.0).astype(BF16)
    frames = frames_ref[:, 0:used, :].reshape(groups * used, part)
    pooled = (dot(picks, frames) / length).astype(BF16)
    clips_ref[...] = pooled
    count, chunk = len(line_refs), line_refs[0].shape[0]
    for k, ref in enumerate(line_refs):
        to = pl.ds(pl.multiple_of(lax.rem(z_ref[0] + count - k, count) * chunk, chunk), chunk)
        embed_ref[to, :] = dot_nt(ref[...], pooled)


def cov_kernel(
    d_ref, x_ref, y_ref, own_ref, other_ref, cols_ref, cols_other_ref, plane0, plane1, plane2, plane3, out_ref
):
    d, x, y = d_ref[0], x_ref[0], y_ref[0]
    clips, part = own_ref.shape
    share = out_ref.shape[1]
    own, other = own_ref[...], other_ref[...]

    def center(embed):
        return embed - jnp.mean(embed, axis=1, keepdims=True)

    cols_high, cols_low = split2(center(cols_ref[...] + cols_other_ref[...]))
    for j, ref in enumerate((plane0, plane1, plane2, plane3)):
        embed = dot_nt(ref[:, half(d, part)], own) + dot_nt(ref[:, half(1 - d, part)], other)
        rows_high, rows_low = split2(center(embed) / (clips - 1))
        block = dot_nt(rows_high, cols_high) + dot_nt(rows_high, cols_low) + dot_nt(rows_low, cols_high)
        for i in range(4):
            peer = 4 * lax.rem(x + 4 - i, 4) + lax.rem(y + 4 - j, 4)
            out_ref[peer] = block[i * share : (i + 1) * share].astype(BF16)


def place_kernel(in_ref, out_ref):
    peers, share, wide = in_ref.shape
    for k in range(peers):
        out_ref[:, k * wide : (k + 1) * wide] = in_ref[k].astype(F32)


SCALAR = pl.BlockSpec(memory_space=pltpu.SMEM)


def per_device(
    tokens,
    router_weight,
    gate_weight,
    up_weight,
    down_weight,
    expand_weight,
    expert_ids,
    frame_slot,
):
    tok_rows, width = tokens.shape
    experts = router_weight.shape[1]
    n_expert = lax.axis_size(EXP)
    n_z = lax.axis_size("z")
    n_xy = n_expert // n_z
    capacity = 4 * tok_rows // experts
    part = width // 2
    hidden = gate_weight.shape[2]
    rows = n_expert * capacity
    count = frame_slot.shape[0]
    frame_total = count * n_expert
    clip_total = frame_total // 4
    share = expand_weight.shape[1]
    d, x, y, z = (lax.axis_index(axis).astype(jnp.int32).reshape(1) for axis in ("dp", "x", "y", "z"))
    swap = [(0, 1), (1, 0)]
    params = pltpu.CompilerParams(vmem_limit_bytes=16 * 2**20)

    mine = expand_weight.T

    def ring(block, axis, step):
        size = lax.axis_size(axis)
        return lax.ppermute(block, axis, [(k, (k + step) % size) for k in range(size)])

    row = jnp.concatenate([mine] + [ring(mine, "x", step) for step in (1, 2, 3)], axis=0)
    planes = [row] + [ring(row, "y", step) for step in (1, 2, 3)]
    first, second = mine[:, :part], mine[:, part:]
    kept = jnp.where(d[0] == 0, first, second)
    sent = lax.ppermute(jnp.where(d[0] == 0, second, first), "dp", swap)
    both = jnp.concatenate(
        [jnp.where(d[0] == 0, kept, sent), jnp.where(d[0] == 0, sent, kept)], axis=0
    )
    along = {step: ring(both, "z", step) for step in (1, 7, 2, 6)}
    with_dispatch = (row, *(along[step] for step in (1, 7)), both)
    with_return = (*planes[1:], *(along[step] for step in (2, 6)))

    vmem = pl.BlockSpec(memory_space=pltpu.VMEM)
    hbm = pl.BlockSpec(memory_space=pl.ANY)
    outgoing, high, low = pl.pallas_call(
        functools.partial(prep_kernel, capacity),
        out_shape=(
            jax.ShapeDtypeStruct((rows, part), BF16),
            jax.ShapeDtypeStruct((rows, tok_rows), BF16),
            jax.ShapeDtypeStruct((rows, tok_rows), BF16),
        ),
        in_specs=[SCALAR, hbm, hbm, hbm],
        out_specs=(vmem, vmem, vmem),
        scratch_shapes=[
            pltpu.VMEM(tokens.shape, BF16),
            pltpu.VMEM((experts, width), BF16),
            pltpu.VMEM((2, tok_rows), jnp.int32),
            pltpu.SemaphoreType.DMA((3,)),
        ],
        compiler_params=pltpu.CompilerParams(vmem_limit_bytes=57 * 2**20),
        name="prep",
    )(d, tokens, router_weight.T, expert_ids.T)

    received = lax.all_to_all(
        outgoing.reshape(n_expert, capacity, part), EXP, split_axis=0, concat_axis=0, tiled=True
    ).reshape(rows, part)
    received = pl.pallas_call(
        order_kernel,
        out_shape=jax.ShapeDtypeStruct((rows, part), BF16),
        in_specs=[hbm] * (1 + len(with_dispatch)),
        out_specs=hbm,
        input_output_aliases={0: 0},
        compiler_params=pltpu.CompilerParams(vmem_limit_bytes=2**20),
        name="order",
    )(received, *with_dispatch)
    other = lax.ppermute(received, "dp", swap)

    w_down = down_weight.reshape(hidden, width)
    inner, theirs = pl.pallas_call(
        functools.partial(ffn_kernel, 512),
        out_shape=(
            jax.ShapeDtypeStruct((rows, hidden), BF16),
            jax.ShapeDtypeStruct((rows, part), BF16),
        ),
        in_specs=[SCALAR, vmem, vmem, hbm, hbm, hbm],
        out_specs=(vmem, vmem),
        scratch_shapes=[
            pltpu.VMEM((rows, width), BF16),
            pltpu.VMEM((width, hidden), BF16),
            pltpu.VMEM((width, hidden), BF16),
            pltpu.VMEM((hidden, width), BF16),
            pltpu.SemaphoreType.DMA((2, 4)),
            pltpu.SemaphoreType.DMA(()),
        ],
        compiler_params=pltpu.CompilerParams(vmem_limit_bytes=48 * 2**20),
        cost_estimate=pl.CostEstimate(
            flops=2 * rows * hidden * (2 * width + part), bytes_accessed=0, transcendentals=0
        ),
        name="ffn",
    )(d, received, other, gate_weight.reshape(width, hidden), up_weight.reshape(width, hidden), w_down)

    brought = lax.ppermute(theirs, "dp", swap)
    ours = pl.pallas_call(
        own_kernel,
        out_shape=jax.ShapeDtypeStruct((rows, part), F32),
        in_specs=[SCALAR, vmem, vmem],
        out_specs=vmem,
        compiler_params=params,
        cost_estimate=pl.CostEstimate(flops=2 * rows * hidden * part, bytes_accessed=0, transcendentals=0),
        name="ours",
    )(d, inner, w_down)
    summed = pl.pallas_call(
        add_kernel,
        out_shape=jax.ShapeDtypeStruct((rows, part), BF16),
        in_specs=[vmem, vmem],
        out_specs=vmem,
        compiler_params=params,
        name="total",
    )(ours, brought)
    back = lax.all_to_all(
        summed.reshape(n_expert, capacity, part), EXP, split_axis=0, concat_axis=0, tiled=True
    ).reshape(rows, part)

    mixed, payload = pl.pallas_call(
        combine_kernel,
        out_shape=(
            jax.ShapeDtypeStruct((tok_rows, part), BF16),
            jax.ShapeDtypeStruct((n_z, 2 * count, part), BF16),
        ),
        in_specs=[SCALAR] * 2 + [vmem] * 5 + [hbm] * len(with_return),
        out_specs=(vmem, vmem),
        compiler_params=params,
        name="combine",
    )(d, z, back, high, low, tokens, frame_slot.reshape(count, 1), *with_return)

    got = lax.all_to_all(payload, "z", split_axis=0, concat_axis=0, tiled=True)
    used = n_z * count
    wide = n_z * 2 * share
    packed = jnp.concatenate(
        [got[:, :count].reshape(used, part), jnp.sum(got[:, count:], axis=0)], axis=0
    )
    line = [both] + [along[step] if step in along else ring(both, "z", step) for step in range(1, n_z)]
    copies = jnp.broadcast_to(packed[None], (n_xy,) + packed.shape)
    gathered = lax.all_to_all(copies, PLANE, split_axis=0, concat_axis=0, tiled=True)
    digits = gathered[:, used, : 2 * used].reshape(n_xy, n_z, 2, count)
    digits = digits.transpose(2, 0, 1, 3).reshape(2, frame_total)
    clips, embed = pl.pallas_call(
        functools.partial(clip_kernel, 4, used),
        out_shape=(
            jax.ShapeDtypeStruct((clip_total, part), BF16),
            jax.ShapeDtypeStruct((wide, clip_total), F32),
        ),
        in_specs=[SCALAR] + [vmem] * (2 + n_z),
        out_specs=(vmem, vmem),
        compiler_params=params,
        name="clips",
    )(z, gathered, digits, *line)
    other_clips = lax.ppermute(clips, "dp", swap)
    other_embed = lax.ppermute(embed, "dp", swap)

    blocks = pl.pallas_call(
        cov_kernel,
        out_shape=jax.ShapeDtypeStruct((n_xy, share, wide), BF16),
        in_specs=[SCALAR] * 3 + [vmem] * 8,
        out_specs=vmem,
        compiler_params=params,
        name="covariance",
    )(d, x, y, clips, other_clips, embed, other_embed, *planes)
    home = lax.all_to_all(blocks, PLANE, split_axis=0, concat_axis=0, tiled=True)
    covariance = pl.pallas_call(
        place_kernel,
        out_shape=jax.ShapeDtypeStruct((share, n_xy * wide), F32),
        in_specs=[vmem],
        out_specs=vmem,
        compiler_params=params,
        name="place",
    )(home)
    return mixed, covariance


def solution(mesh):
    grid = Mesh(mesh.devices.reshape(4, 4, 8, 2), ALL)
    return jax.shard_map(
        per_device,
        mesh=grid,
        in_specs=(
            P(EXP, None),
            P(),
            P(EXP, None, "dp"),
            P(EXP, None, "dp"),
            P(EXP, "dp", None),
            P(None, ALL),
            P(EXP, None),
            P(EXP),
        ),
        out_specs=(P(EXP, "dp"), P(ALL, None)),
        check_vma=False,
    )
```

```python
import functools

import jax
import jax.numpy as jnp
from jax import lax
from jax.experimental import pallas as pl
from jax.experimental.pallas import tpu as pltpu
from jax.sharding import Mesh, PartitionSpec as P

EXP = ("x", "y", "z")
ALL = ("x", "y", "z", "dp")
PLANE = ("x", "y")
F32 = jnp.float32
BF16 = jnp.bfloat16
LANES = 128
NT = (((1,), (1,)), ((), ()))
TN = (((0,), (0,)), ((), ()))


def dot(a, b):
    return jnp.dot(a, b, preferred_element_type=F32)


def dot_nt(a, b):
    return lax.dot_general(a, b, NT, preferred_element_type=F32)


def dot_tn(a, b):
    return lax.dot_general(a, b, TN, preferred_element_type=F32)


def split2(v):
    high = v.astype(BF16)
    return high, (v - high.astype(F32)).astype(BF16)


def half(start, size):
    return pl.ds(pl.multiple_of(start * size, LANES), size)


def slots_taken(ids_ref, shape):
    experts, rows, capacity = shape
    number = lax.broadcasted_iota(jnp.int32, (experts, rows), 0)
    hot0 = ids_ref[0:1, :] == number
    hot1 = ids_ref[1:2, :] == number
    member = jnp.where(hot0 | hot1, 1.0, 0.0)
    before = lax.broadcasted_iota(jnp.int32, (rows, rows), 0) < lax.broadcasted_iota(
        jnp.int32, (rows, rows), 1
    )
    earlier = dot(member.astype(BF16), jnp.where(before, 1.0, 0.0).astype(BF16))
    place = jnp.where(member > 0.0, earlier, -1.0)
    slots = lax.broadcasted_iota(jnp.int32, (experts, 2, capacity, rows), 2).astype(F32)
    return hot0, hot1, place[:, None, None, :] == slots


def prep_kernel(experts, capacity, d_ref, tok_hbm, ids_hbm, out_ref, tok_ref, ids_ref, sems):
    copies = [
        pltpu.make_async_copy(source, target, sems.at[k])
        for k, (source, target) in enumerate(((ids_hbm, ids_ref), (tok_hbm, tok_ref)))
    ]
    for copy in copies:
        copy.start()
    d = d_ref[0]
    rows, width = tok_ref.shape
    copies[0].wait()
    _, _, taken = slots_taken(ids_ref, (experts, rows, capacity))
    picks = jnp.where(taken, 1.0, 0.0).reshape(experts * 2 * capacity, rows).astype(BF16)
    copies[1].wait()
    out_ref[...] = dot(picks, tok_ref[:, half(d, width // 2)]).astype(BF16)


def gate_kernel(capacity, tok_ref, router_ref, ids_ref, high_ref, low_ref):
    rows = tok_ref.shape[0]
    experts = router_ref.shape[0]
    logits = dot_nt(router_ref[...], tok_ref[...])
    hot0, hot1, taken = slots_taken(ids_ref, (experts, rows, capacity))
    chosen0 = jnp.sum(jnp.where(hot0, logits, 0.0), axis=0, keepdims=True)
    chosen1 = jnp.sum(jnp.where(hot1, logits, 0.0), axis=0, keepdims=True)
    gate = jnp.where(hot0, jax.nn.sigmoid(chosen0 - chosen1), 0.0) + jnp.where(
        hot1, jax.nn.sigmoid(chosen1 - chosen0), 0.0
    )
    weights = jnp.where(taken, gate[:, None, None, :], 0.0).reshape(experts * 2 * capacity, rows)
    high_ref[...], low_ref[...] = split2(weights)


def order_kernel(*refs):
    pass


def ffn_kernel(
    step, d_ref, own_ref, other_ref, gate_hbm, up_hbm, down_hbm, hid_ref, out_ref, x_ref, gate_ref, up_ref, down_ref, sems, down_sem
):
    d = d_ref[0]
    rows, part = own_ref.shape
    blocks = sems.shape[1]
    block = gate_ref.shape[1] // blocks
    spans = [slice(k * block, (k + 1) * block) for k in range(blocks)]
    loads = [
        [
            pltpu.make_async_copy(source.at[:, span], target.at[:, span], sems.at[w, k])
            for w, (source, target) in enumerate(((gate_hbm, gate_ref), (up_hbm, up_ref)))
        ]
        for k, span in enumerate(spans)
    ]
    load_down = pltpu.make_async_copy(down_hbm, down_ref, down_sem)
    for pair in loads:
        for load in pair:
            load.start()
    load_down.start()
    x_ref[:, half(d, part)] = own_ref[...]
    x_ref[:, half(1 - d, part)] = other_ref[...]

    steps = [slice(m * step, (m + 1) * step) for m in range(rows // step)]
    for pair, span in zip(loads, spans):
        for load in pair:
            load.wait()
        for at in steps:
            gate = dot(x_ref[at, :], gate_ref[:, span])
            upper = dot(x_ref[at, :], up_ref[:, span])
            hid_ref[at, span] = (gate * jax.nn.sigmoid(gate) * upper).astype(BF16)
    load_down.wait()
    for at in steps:
        out_ref[at, :] = dot(hid_ref[at, :], down_ref[:, half(1 - d, part)]).astype(BF16)


def own_kernel(d_ref, hid_ref, down_ref, out_ref):
    out_ref[...] = dot(hid_ref[...], down_ref[:, half(d_ref[0], out_ref.shape[1])])


def add_kernel(own_ref, brought_ref, out_ref):
    out_ref[...] = (own_ref[...] + brought_ref[...].astype(F32)).astype(BF16)


def combine_kernel(d_ref, z_ref, back_ref, high_ref, low_ref, tok_ref, slot_ref, *refs):
    mixed_ref, payload_ref = refs[-2:]
    d, z = d_ref[0], z_ref[0]
    rows, part = mixed_ref.shape
    count = slot_ref.shape[0]
    back = back_ref[...]
    moe = dot_tn(high_ref[...], back) + dot_tn(low_ref[...], back)
    mixed = (tok_ref[:, half(d, part)].astype(F32) + moe).astype(BF16)
    mixed_ref[...] = mixed
    length = rows // count
    frames = jnp.sum(mixed.astype(F32).reshape(count, length, part), axis=1) / length
    slot = slot_ref[...]
    lane = lax.broadcasted_iota(jnp.int32, (count, part), 1)
    number = lax.broadcasted_iota(jnp.int32, (count, part), 0)
    digit = jnp.where(lane % (2 * count) < count, slot // 32, slot % 32)
    here = (lane // (2 * count) == z) & (lane % count == number)
    digits = jnp.sum(jnp.where(here, digit, 0).astype(F32), axis=0, keepdims=True)
    first = jnp.where(number == 0, jnp.broadcast_to(digits, (count, part)), 0.0)
    block = jnp.concatenate([frames, first], axis=0).astype(BF16)
    for k in range(payload_ref.shape[0]):
        payload_ref[k] = block


def clip_kernel(length, used, frames_ref, digits_ref, clips_ref):
    clips, part = clips_ref.shape
    groups = frames_ref.shape[0]
    digits = digits_ref[...].astype(F32)
    slot = digits[0:1, :] * 32.0 + digits[1:2, :]
    clip = jnp.floor(slot / length)
    number = lax.broadcasted_iota(jnp.int32, (clips, groups * used), 0).astype(F32)
    picks = jnp.where(clip == number, 1.0, 0.0).astype(BF16)
    frames = frames_ref[:, 0:used, :].reshape(groups * used, part)
    pooled = (dot(picks, frames) / length).astype(BF16)
    clips_ref[...] = pooled


def line_kernel(z_ref, clips_ref, *refs):
    line_refs, embed_ref = refs[:-1], refs[-1]
    pooled = clips_ref[...]
    count, chunk = len(line_refs), line_refs[0].shape[0]
    embed = dot_nt(jnp.concatenate([ref[...] for ref in line_refs], axis=0), pooled)
    for k in range(count):
        to = pl.ds(pl.multiple_of(lax.rem(z_ref[0] + count - k, count) * chunk, chunk), chunk)
        embed_ref[to, :] = embed[k * chunk : (k + 1) * chunk]


def cov_kernel(
    d_ref, x_ref, y_ref, own_ref, other_ref, cols_ref, cols_other_ref, plane0, plane1, plane2, plane3, out_ref
):
    d, x, y = d_ref[0], x_ref[0], y_ref[0]
    clips, part = own_ref.shape
    share = out_ref.shape[1]
    own, other = own_ref[...], other_ref[...]

    def center(embed):
        return embed - jnp.mean(embed, axis=1, keepdims=True)

    cols_high, cols_low = split2(center(cols_ref[...] + cols_other_ref[...]))
    planes = (plane0, plane1, plane2, plane3)
    mine = jnp.concatenate([ref[:, half(d, part)] for ref in planes], axis=0)
    theirs = jnp.concatenate([ref[:, half(1 - d, part)] for ref in planes], axis=0)
    rows_high, rows_low = split2(center(dot_nt(mine, own) + dot_nt(theirs, other)) / (clips - 1))
    block = dot_nt(rows_high, cols_high) + dot_nt(rows_high, cols_low) + dot_nt(rows_low, cols_high)
    block = block.astype(BF16)
    for j in range(4):
        for i in range(4):
            peer = 4 * lax.rem(x + 4 - i, 4) + lax.rem(y + 4 - j, 4)
            k = 4 * j + i
            out_ref[peer] = block[k * share : (k + 1) * share]


def place_kernel(in_ref, out_ref):
    peers, share, wide = in_ref.shape
    for k in range(peers):
        out_ref[:, k * wide : (k + 1) * wide] = in_ref[k].astype(F32)


SCALAR = pl.BlockSpec(memory_space=pltpu.SMEM)


def per_device(
    tokens,
    router_weight,
    gate_weight,
    up_weight,
    down_weight,
    expand_weight,
    expert_ids,
    frame_slot,
):
    tok_rows, width = tokens.shape
    experts = router_weight.shape[1]
    n_expert = lax.axis_size(EXP)
    n_z = lax.axis_size("z")
    n_xy = n_expert // n_z
    capacity = 4 * tok_rows // experts
    part = width // 2
    hidden = gate_weight.shape[2]
    rows = n_expert * capacity
    count = frame_slot.shape[0]
    frame_total = count * n_expert
    clip_total = frame_total // 4
    share = expand_weight.shape[1]
    d, x, y, z = (lax.axis_index(axis).astype(jnp.int32).reshape(1) for axis in ("dp", "x", "y", "z"))
    swap = [(0, 1), (1, 0)]
    params = pltpu.CompilerParams(vmem_limit_bytes=16 * 2**20)

    mine = expand_weight.T

    def ring(block, axis, step):
        size = lax.axis_size(axis)
        return lax.ppermute(block, axis, [(k, (k + step) % size) for k in range(size)])

    row = jnp.concatenate([mine] + [ring(mine, "x", step) for step in (1, 2, 3)], axis=0)
    planes = [row] + [ring(row, "y", step) for step in (1, 2, 3)]
    first, second = mine[:, :part], mine[:, part:]
    kept = jnp.where(d[0] == 0, first, second)
    sent = lax.ppermute(jnp.where(d[0] == 0, second, first), "dp", swap)
    both = jnp.concatenate(
        [jnp.where(d[0] == 0, kept, sent), jnp.where(d[0] == 0, sent, kept)], axis=0
    )
    along = {step: ring(both, "z", step) for step in (1, 7, 2, 6)}
    with_dispatch = (row, *(along[step] for step in (1, 7)), both)
    with_return = (*planes[1:], *(along[step] for step in (2, 6)))

    vmem = pl.BlockSpec(memory_space=pltpu.VMEM)
    hbm = pl.BlockSpec(memory_space=pl.ANY)
    outgoing = pl.pallas_call(
        functools.partial(prep_kernel, experts, capacity),
        out_shape=jax.ShapeDtypeStruct((rows, part), BF16),
        in_specs=[SCALAR, hbm, hbm],
        out_specs=vmem,
        scratch_shapes=[
            pltpu.VMEM(tokens.shape, BF16),
            pltpu.VMEM((2, tok_rows), jnp.int32),
            pltpu.SemaphoreType.DMA((2,)),
        ],
        compiler_params=pltpu.CompilerParams(vmem_limit_bytes=57 * 2**20),
        name="prep",
    )(d, tokens, expert_ids.T)
    high, low = pl.pallas_call(
        functools.partial(gate_kernel, capacity),
        out_shape=[jax.ShapeDtypeStruct((rows, tok_rows), BF16)] * 2,
        in_specs=[vmem] * 3,
        out_specs=(vmem, vmem),
        compiler_params=params,
        cost_estimate=pl.CostEstimate(
            flops=2 * tok_rows * width * experts, bytes_accessed=0, transcendentals=0
        ),
        name="gates",
    )(tokens, router_weight.T, expert_ids.T)

    received = lax.all_to_all(
        outgoing.reshape(n_expert, capacity, part), EXP, split_axis=0, concat_axis=0, tiled=True
    ).reshape(rows, part)
    with_dispatch = (high, low, *with_dispatch)
    received = pl.pallas_call(
        order_kernel,
        out_shape=jax.ShapeDtypeStruct((rows, part), BF16),
        in_specs=[hbm] * (1 + len(with_dispatch)),
        out_specs=hbm,
        input_output_aliases={0: 0},
        compiler_params=pltpu.CompilerParams(vmem_limit_bytes=2**20),
        name="order",
    )(received, *with_dispatch)
    other = lax.ppermute(received, "dp", swap)

    w_down = down_weight.reshape(hidden, width)
    inner, theirs = pl.pallas_call(
        functools.partial(ffn_kernel, 512),
        out_shape=(
            jax.ShapeDtypeStruct((rows, hidden), BF16),
            jax.ShapeDtypeStruct((rows, part), BF16),
        ),
        in_specs=[SCALAR, vmem, vmem, hbm, hbm, hbm],
        out_specs=(vmem, vmem),
        scratch_shapes=[
            pltpu.VMEM((rows, width), BF16),
            pltpu.VMEM((width, hidden), BF16),
            pltpu.VMEM((width, hidden), BF16),
            pltpu.VMEM((hidden, width), BF16),
            pltpu.SemaphoreType.DMA((2, 4)),
            pltpu.SemaphoreType.DMA(()),
        ],
        compiler_params=pltpu.CompilerParams(vmem_limit_bytes=48 * 2**20),
        cost_estimate=pl.CostEstimate(
            flops=2 * rows * hidden * (2 * width + part), bytes_accessed=0, transcendentals=0
        ),
        name="ffn",
    )(d, received, other, gate_weight.reshape(width, hidden), up_weight.reshape(width, hidden), w_down)

    brought = lax.ppermute(theirs, "dp", swap)
    ours = pl.pallas_call(
        own_kernel,
        out_shape=jax.ShapeDtypeStruct((rows, part), F32),
        in_specs=[SCALAR, vmem, vmem],
        out_specs=vmem,
        compiler_params=params,
        cost_estimate=pl.CostEstimate(flops=2 * rows * hidden * part, bytes_accessed=0, transcendentals=0),
        name="ours",
    )(d, inner, w_down)
    summed = pl.pallas_call(
        add_kernel,
        out_shape=jax.ShapeDtypeStruct((rows, part), BF16),
        in_specs=[vmem, vmem],
        out_specs=vmem,
        compiler_params=params,
        name="total",
    )(ours, brought)
    back = lax.all_to_all(
        summed.reshape(n_expert, capacity, part), EXP, split_axis=0, concat_axis=0, tiled=True
    ).reshape(rows, part)

    mixed, payload = pl.pallas_call(
        combine_kernel,
        out_shape=(
            jax.ShapeDtypeStruct((tok_rows, part), BF16),
            jax.ShapeDtypeStruct((n_z, 2 * count, part), BF16),
        ),
        in_specs=[SCALAR] * 2 + [vmem] * 5 + [hbm] * len(with_return),
        out_specs=(vmem, vmem),
        compiler_params=params,
        name="combine",
    )(d, z, back, high, low, tokens, frame_slot.reshape(count, 1), *with_return)

    got = lax.all_to_all(payload, "z", split_axis=0, concat_axis=0, tiled=True)
    used = n_z * count
    wide = n_z * 2 * share
    packed = jnp.concatenate(
        [got[:, :count].reshape(used, part), jnp.sum(got[:, count:], axis=0)], axis=0
    )
    line = [both] + [along[step] if step in along else ring(both, "z", step) for step in range(1, n_z)]
    copies = jnp.broadcast_to(packed[None], (n_xy,) + packed.shape)
    gathered = lax.all_to_all(copies, PLANE, split_axis=0, concat_axis=0, tiled=True)
    digits = gathered[:, used, : 2 * used].reshape(n_xy, n_z, 2, count)
    digits = digits.transpose(2, 0, 1, 3).reshape(2, frame_total)
    clips = pl.pallas_call(
        functools.partial(clip_kernel, 4, used),
        out_shape=jax.ShapeDtypeStruct((clip_total, part), BF16),
        in_specs=[vmem, vmem],
        out_specs=vmem,
        compiler_params=params,
        name="clips",
    )(gathered, digits)
    other_clips = lax.ppermute(clips, "dp", swap)
    embed = pl.pallas_call(
        line_kernel,
        out_shape=jax.ShapeDtypeStruct((wide, clip_total), F32),
        in_specs=[SCALAR] + [vmem] * (1 + n_z),
        out_specs=vmem,
        compiler_params=params,
        cost_estimate=pl.CostEstimate(
            flops=2 * wide * part * clip_total, bytes_accessed=0, transcendentals=0
        ),
        name="line",
    )(z, clips, *line)
    other_embed = lax.ppermute(embed, "dp", swap)

    blocks = pl.pallas_call(
        cov_kernel,
        out_shape=jax.ShapeDtypeStruct((n_xy, share, wide), BF16),
        in_specs=[SCALAR] * 3 + [vmem] * 8,
        out_specs=vmem,
        compiler_params=params,
        name="covariance",
    )(d, x, y, clips, other_clips, embed, other_embed, *planes)
    home = lax.all_to_all(blocks, PLANE, split_axis=0, concat_axis=0, tiled=True)
    covariance = pl.pallas_call(
        place_kernel,
        out_shape=jax.ShapeDtypeStruct((share, n_xy * wide), F32),
        in_specs=[vmem],
        out_specs=vmem,
        compiler_params=params,
        name="place",
    )(home)
    return mixed, covariance


def solution(mesh):
    grid = Mesh(mesh.devices.reshape(4, 4, 8, 2), ALL)
    return jax.shard_map(
        per_device,
        mesh=grid,
        in_specs=(
            P(EXP, None),
            P(),
            P(EXP, None, "dp"),
            P(EXP, None, "dp"),
            P(EXP, "dp", None),
            P(None, ALL),
            P(EXP, None),
            P(EXP),
        ),
        out_specs=(P(EXP, "dp"), P(ALL, None)),
        check_vma=False,
    )
```

```python
import functools

import jax
import jax.numpy as jnp
from jax import lax
from jax.experimental import pallas as pl
from jax.experimental.pallas import tpu as pltpu
from jax.sharding import Mesh, PartitionSpec as P

EXP = ("x", "y", "z")
ALL = ("x", "y", "z", "dp")
PLANE = ("x", "y")
F32 = jnp.float32
BF16 = jnp.bfloat16
LANES = 128
NT = (((1,), (1,)), ((), ()))
TN = (((0,), (0,)), ((), ()))


def dot(a, b):
    return jnp.dot(a, b, preferred_element_type=F32)


def dot_nt(a, b):
    return lax.dot_general(a, b, NT, preferred_element_type=F32)


def dot_tn(a, b):
    return lax.dot_general(a, b, TN, preferred_element_type=F32)


def split2(v):
    high = v.astype(BF16)
    return high, (v - high.astype(F32)).astype(BF16)


def half(start, size):
    return pl.ds(pl.multiple_of(start * size, LANES), size)


def slots_taken(ids_ref, shape):
    experts, rows, capacity = shape
    number = lax.broadcasted_iota(jnp.int32, (experts, rows), 0)
    hot0 = ids_ref[0:1, :] == number
    hot1 = ids_ref[1:2, :] == number
    member = jnp.where(hot0 | hot1, 1.0, 0.0)
    before = lax.broadcasted_iota(jnp.int32, (rows, rows), 0) < lax.broadcasted_iota(
        jnp.int32, (rows, rows), 1
    )
    earlier = dot(member.astype(BF16), jnp.where(before, 1.0, 0.0).astype(BF16))
    place = jnp.where(member > 0.0, earlier, -1.0)
    slots = lax.broadcasted_iota(jnp.int32, (experts, 2, capacity, rows), 2).astype(F32)
    return hot0, hot1, place[:, None, None, :] == slots


def prep_kernel(experts, capacity, d_ref, tok_hbm, ids_hbm, out_ref, tok_ref, ids_ref, sems):
    copies = [
        pltpu.make_async_copy(source, target, sems.at[k])
        for k, (source, target) in enumerate(((ids_hbm, ids_ref), (tok_hbm, tok_ref)))
    ]
    for copy in copies:
        copy.start()
    d = d_ref[0]
    rows, width = tok_ref.shape
    copies[0].wait()
    _, _, taken = slots_taken(ids_ref, (experts, rows, capacity))
    picks = jnp.where(taken, 1.0, 0.0).reshape(experts * 2 * capacity, rows).astype(BF16)
    copies[1].wait()
    out_ref[...] = dot(picks, tok_ref[:, half(d, width // 2)]).astype(BF16)


def gate_kernel(capacity, tok_ref, router_ref, ids_ref, high_ref, low_ref):
    rows = tok_ref.shape[0]
    experts = router_ref.shape[0]
    logits = dot_nt(router_ref[...], tok_ref[...])
    hot0, hot1, taken = slots_taken(ids_ref, (experts, rows, capacity))
    chosen0 = jnp.sum(jnp.where(hot0, logits, 0.0), axis=0, keepdims=True)
    chosen1 = jnp.sum(jnp.where(hot1, logits, 0.0), axis=0, keepdims=True)
    gate = jnp.where(hot0, jax.nn.sigmoid(chosen0 - chosen1), 0.0) + jnp.where(
        hot1, jax.nn.sigmoid(chosen1 - chosen0), 0.0
    )
    weights = jnp.where(taken, gate[:, None, None, :], 0.0).reshape(experts * 2 * capacity, rows)
    high_ref[...], low_ref[...] = split2(weights)


def order_kernel(*refs):
    pass


def load_kernel(gate_hbm, up_hbm, after_hbm, gate_ref, up_ref, sems):
    copies = [
        pltpu.make_async_copy(source, target, sems.at[k])
        for k, (source, target) in enumerate(((gate_hbm, gate_ref), (up_hbm, up_ref)))
    ]
    for copy in copies:
        copy.start()
    for copy in copies:
        copy.wait()


def ffn_kernel(
    step, block, d_ref, own_ref, other_ref, gate_ref, up_ref, down_hbm, hid_ref, out_ref, x_ref, down_ref, sem
):
    d = d_ref[0]
    rows, part = own_ref.shape
    load_down = pltpu.make_async_copy(down_hbm, down_ref, sem)
    load_down.start()
    x_ref[:, half(d, part)] = own_ref[...]
    x_ref[:, half(1 - d, part)] = other_ref[...]
    steps = [slice(m * step, (m + 1) * step) for m in range(rows // step)]
    for j in range(gate_ref.shape[1] // block):
        span = slice(j * block, (j + 1) * block)
        for at in steps:
            gate = dot(x_ref[at, :], gate_ref[:, span])
            upper = dot(x_ref[at, :], up_ref[:, span])
            hid_ref[at, span] = (gate * jax.nn.sigmoid(gate) * upper).astype(BF16)
    load_down.wait()
    for at in steps:
        out_ref[at, :] = dot(hid_ref[at, :], down_ref[:, half(1 - d, part)]).astype(BF16)


def own_kernel(d_ref, hid_ref, down_ref, out_ref):
    out_ref[...] = dot(hid_ref[...], down_ref[:, half(d_ref[0], out_ref.shape[1])])


def add_kernel(own_ref, brought_ref, out_ref):
    out_ref[...] = (own_ref[...] + brought_ref[...].astype(F32)).astype(BF16)


def combine_kernel(d_ref, z_ref, back_ref, high_ref, low_ref, tok_ref, slot_ref, *refs):
    mixed_ref, payload_ref = refs[-2:]
    d, z = d_ref[0], z_ref[0]
    rows, part = mixed_ref.shape
    count = slot_ref.shape[0]
    back = back_ref[...]
    moe = dot_tn(high_ref[...], back) + dot_tn(low_ref[...], back)
    mixed = (tok_ref[:, half(d, part)].astype(F32) + moe).astype(BF16)
    mixed_ref[...] = mixed
    length = rows // count
    frames = jnp.sum(mixed.astype(F32).reshape(count, length, part), axis=1) / length
    slot = slot_ref[...]
    lane = lax.broadcasted_iota(jnp.int32, (count, part), 1)
    number = lax.broadcasted_iota(jnp.int32, (count, part), 0)
    digit = jnp.where(lane % (2 * count) < count, slot // 32, slot % 32)
    here = (lane // (2 * count) == z) & (lane % count == number)
    digits = jnp.sum(jnp.where(here, digit, 0).astype(F32), axis=0, keepdims=True)
    first = jnp.where(number == 0, jnp.broadcast_to(digits, (count, part)), 0.0)
    block = jnp.concatenate([frames, first], axis=0).astype(BF16)
    for k in range(payload_ref.shape[0]):
        payload_ref[k] = block


def clip_kernel(length, used, frames_ref, digits_ref, clips_ref):
    clips, part = clips_ref.shape
    groups = frames_ref.shape[0]
    digits = digits_ref[...].astype(F32)
    slot = digits[0:1, :] * 32.0 + digits[1:2, :]
    clip = jnp.floor(slot / length)
    number = lax.broadcasted_iota(jnp.int32, (clips, groups * used), 0).astype(F32)
    picks = jnp.where(clip == number, 1.0, 0.0).astype(BF16)
    frames = frames_ref[:, 0:used, :].reshape(groups * used, part)
    pooled = (dot(picks, frames) / length).astype(BF16)
    clips_ref[...] = pooled


def line_kernel(z_ref, clips_ref, *refs):
    line_refs, embed_ref = refs[:-1], refs[-1]
    pooled = clips_ref[...]
    count, chunk = len(line_refs), line_refs[0].shape[0]
    embed = dot_nt(jnp.concatenate([ref[...] for ref in line_refs], axis=0), pooled)
    for k in range(count):
        to = pl.ds(pl.multiple_of(lax.rem(z_ref[0] + count - k, count) * chunk, chunk), chunk)
        embed_ref[to, :] = embed[k * chunk : (k + 1) * chunk]


def cov_kernel(
    d_ref, x_ref, y_ref, own_ref, other_ref, cols_ref, cols_other_ref, plane0, plane1, plane2, plane3, out_ref
):
    d, x, y = d_ref[0], x_ref[0], y_ref[0]
    clips, part = own_ref.shape
    share = out_ref.shape[1]
    own, other = own_ref[...], other_ref[...]

    def center(embed):
        return embed - jnp.mean(embed, axis=1, keepdims=True)

    cols_high, cols_low = split2(center(cols_ref[...] + cols_other_ref[...]))
    planes = (plane0, plane1, plane2, plane3)
    mine = jnp.concatenate([ref[:, half(d, part)] for ref in planes], axis=0)
    theirs = jnp.concatenate([ref[:, half(1 - d, part)] for ref in planes], axis=0)
    rows_high, rows_low = split2(center(dot_nt(mine, own) + dot_nt(theirs, other)) / (clips - 1))
    block = dot_nt(rows_high, cols_high) + dot_nt(rows_high, cols_low) + dot_nt(rows_low, cols_high)
    block = block.astype(BF16)
    for j in range(4):
        for i in range(4):
            peer = 4 * lax.rem(x + 4 - i, 4) + lax.rem(y + 4 - j, 4)
            k = 4 * j + i
            out_ref[peer] = block[k * share : (k + 1) * share]


def place_kernel(in_ref, out_ref):
    peers, share, wide = in_ref.shape
    for k in range(peers):
        out_ref[:, k * wide : (k + 1) * wide] = in_ref[k].astype(F32)


SCALAR = pl.BlockSpec(memory_space=pltpu.SMEM)


def per_device(
    tokens,
    router_weight,
    gate_weight,
    up_weight,
    down_weight,
    expand_weight,
    expert_ids,
    frame_slot,
):
    tok_rows, width = tokens.shape
    experts = router_weight.shape[1]
    n_expert = lax.axis_size(EXP)
    n_z = lax.axis_size("z")
    n_xy = n_expert // n_z
    capacity = 4 * tok_rows // experts
    part = width // 2
    hidden = gate_weight.shape[2]
    rows = n_expert * capacity
    count = frame_slot.shape[0]
    frame_total = count * n_expert
    clip_total = frame_total // 4
    share = expand_weight.shape[1]
    d, x, y, z = (lax.axis_index(axis).astype(jnp.int32).reshape(1) for axis in ("dp", "x", "y", "z"))
    swap = [(0, 1), (1, 0)]
    params = pltpu.CompilerParams(vmem_limit_bytes=16 * 2**20)

    mine = expand_weight.T

    def ring(block, axis, step):
        size = lax.axis_size(axis)
        return lax.ppermute(block, axis, [(k, (k + step) % size) for k in range(size)])

    row = jnp.concatenate([mine] + [ring(mine, "x", step) for step in (1, 2, 3)], axis=0)
    planes = [row] + [ring(row, "y", step) for step in (1, 2, 3)]
    first, second = mine[:, :part], mine[:, part:]
    kept = jnp.where(d[0] == 0, first, second)
    sent = lax.ppermute(jnp.where(d[0] == 0, second, first), "dp", swap)
    both = jnp.concatenate(
        [jnp.where(d[0] == 0, kept, sent), jnp.where(d[0] == 0, sent, kept)], axis=0
    )
    along = {step: ring(both, "z", step) for step in (1, 7, 2, 6)}
    with_dispatch = (row, *(along[step] for step in (1, 7)), both)
    with_return = (*planes[1:], *(along[step] for step in (2, 6)))

    vmem = pl.BlockSpec(memory_space=pltpu.VMEM)
    hbm = pl.BlockSpec(memory_space=pl.ANY)
    outgoing = pl.pallas_call(
        functools.partial(prep_kernel, experts, capacity),
        out_shape=jax.ShapeDtypeStruct((rows, part), BF16),
        in_specs=[SCALAR, hbm, hbm],
        out_specs=vmem,
        scratch_shapes=[
            pltpu.VMEM(tokens.shape, BF16),
            pltpu.VMEM((2, tok_rows), jnp.int32),
            pltpu.SemaphoreType.DMA((2,)),
        ],
        compiler_params=pltpu.CompilerParams(vmem_limit_bytes=57 * 2**20),
        name="prep",
    )(d, tokens, expert_ids.T)
    high, low = pl.pallas_call(
        functools.partial(gate_kernel, capacity),
        out_shape=[jax.ShapeDtypeStruct((rows, tok_rows), BF16)] * 2,
        in_specs=[vmem] * 3,
        out_specs=(vmem, vmem),
        compiler_params=params,
        cost_estimate=pl.CostEstimate(
            flops=2 * tok_rows * width * experts, bytes_accessed=0, transcendentals=0
        ),
        name="gates",
    )(tokens, router_weight.T, expert_ids.T)

    received = lax.all_to_all(
        outgoing.reshape(n_expert, capacity, part), EXP, split_axis=0, concat_axis=0, tiled=True
    ).reshape(rows, part)
    with_dispatch = (high, low, *with_dispatch)
    received = pl.pallas_call(
        order_kernel,
        out_shape=jax.ShapeDtypeStruct((rows, part), BF16),
        in_specs=[hbm] * (1 + len(with_dispatch)),
        out_specs=hbm,
        input_output_aliases={0: 0},
        compiler_params=pltpu.CompilerParams(vmem_limit_bytes=2**20),
        name="order",
    )(received, *with_dispatch)
    other = lax.ppermute(received, "dp", swap)

    w_down = down_weight.reshape(hidden, width)
    w_gate, w_up = pl.pallas_call(
        load_kernel,
        out_shape=[jax.ShapeDtypeStruct((width, hidden), BF16)] * 2,
        in_specs=[hbm] * 3,
        out_specs=(vmem, vmem),
        scratch_shapes=[pltpu.SemaphoreType.DMA((2,))],
        compiler_params=pltpu.CompilerParams(vmem_limit_bytes=48 * 2**20),
        cost_estimate=pl.CostEstimate(flops=0, bytes_accessed=4 * width * hidden * 2, transcendentals=0),
        name="load",
    )(gate_weight.reshape(width, hidden), up_weight.reshape(width, hidden), received)
    inner, theirs = pl.pallas_call(
        functools.partial(ffn_kernel, 512, 256),
        out_shape=(
            jax.ShapeDtypeStruct((rows, hidden), BF16),
            jax.ShapeDtypeStruct((rows, part), BF16),
        ),
        in_specs=[SCALAR] + [vmem] * 4 + [hbm],
        out_specs=(vmem, vmem),
        scratch_shapes=[
            pltpu.VMEM((rows, width), BF16),
            pltpu.VMEM((hidden, width), BF16),
            pltpu.SemaphoreType.DMA(()),
        ],
        compiler_params=pltpu.CompilerParams(vmem_limit_bytes=40 * 2**20),
        cost_estimate=pl.CostEstimate(
            flops=2 * rows * hidden * (2 * width + part), bytes_accessed=0, transcendentals=0
        ),
        name="ffn",
    )(d, received, other, w_gate, w_up, w_down)

    brought = lax.ppermute(theirs, "dp", swap)
    ours = pl.pallas_call(
        own_kernel,
        out_shape=jax.ShapeDtypeStruct((rows, part), F32),
        in_specs=[SCALAR, vmem, vmem],
        out_specs=vmem,
        compiler_params=params,
        cost_estimate=pl.CostEstimate(flops=2 * rows * hidden * part, bytes_accessed=0, transcendentals=0),
        name="ours",
    )(d, inner, w_down)
    summed = pl.pallas_call(
        add_kernel,
        out_shape=jax.ShapeDtypeStruct((rows, part), BF16),
        in_specs=[vmem, vmem],
        out_specs=vmem,
        compiler_params=params,
        name="total",
    )(ours, brought)
    back = lax.all_to_all(
        summed.reshape(n_expert, capacity, part), EXP, split_axis=0, concat_axis=0, tiled=True
    ).reshape(rows, part)

    mixed, payload = pl.pallas_call(
        combine_kernel,
        out_shape=(
            jax.ShapeDtypeStruct((tok_rows, part), BF16),
            jax.ShapeDtypeStruct((n_z, 2 * count, part), BF16),
        ),
        in_specs=[SCALAR] * 2 + [vmem] * 5 + [hbm] * len(with_return),
        out_specs=(vmem, vmem),
        compiler_params=params,
        name="combine",
    )(d, z, back, high, low, tokens, frame_slot.reshape(count, 1), *with_return)

    got = lax.all_to_all(payload, "z", split_axis=0, concat_axis=0, tiled=True)
    used = n_z * count
    wide = n_z * 2 * share
    packed = jnp.concatenate(
        [got[:, :count].reshape(used, part), jnp.sum(got[:, count:], axis=0)], axis=0
    )
    line = [both] + [along[step] if step in along else ring(both, "z", step) for step in range(1, n_z)]
    copies = jnp.broadcast_to(packed[None], (n_xy,) + packed.shape)
    gathered = lax.all_to_all(copies, PLANE, split_axis=0, concat_axis=0, tiled=True)
    digits = gathered[:, used, : 2 * used].reshape(n_xy, n_z, 2, count)
    digits = digits.transpose(2, 0, 1, 3).reshape(2, frame_total)
    clips = pl.pallas_call(
        functools.partial(clip_kernel, 4, used),
        out_shape=jax.ShapeDtypeStruct((clip_total, part), BF16),
        in_specs=[vmem, vmem],
        out_specs=vmem,
        compiler_params=params,
        name="clips",
    )(gathered, digits)
    other_clips = lax.ppermute(clips, "dp", swap)
    embed = pl.pallas_call(
        line_kernel,
        out_shape=jax.ShapeDtypeStruct((wide, clip_total), F32),
        in_specs=[SCALAR] + [vmem] * (1 + n_z),
        out_specs=vmem,
        compiler_params=params,
        cost_estimate=pl.CostEstimate(
            flops=2 * wide * part * clip_total, bytes_accessed=0, transcendentals=0
        ),
        name="line",
    )(z, clips, *line)
    other_embed = lax.ppermute(embed, "dp", swap)

    blocks = pl.pallas_call(
        cov_kernel,
        out_shape=jax.ShapeDtypeStruct((n_xy, share, wide), BF16),
        in_specs=[SCALAR] * 3 + [vmem] * 8,
        out_specs=vmem,
        compiler_params=params,
        name="covariance",
    )(d, x, y, clips, other_clips, embed, other_embed, *planes)
    home = lax.all_to_all(blocks, PLANE, split_axis=0, concat_axis=0, tiled=True)
    covariance = pl.pallas_call(
        place_kernel,
        out_shape=jax.ShapeDtypeStruct((share, n_xy * wide), F32),
        in_specs=[vmem],
        out_specs=vmem,
        compiler_params=params,
        name="place",
    )(home)
    return mixed, covariance


def solution(mesh):
    grid = Mesh(mesh.devices.reshape(4, 4, 8, 2), ALL)
    return jax.shard_map(
        per_device,
        mesh=grid,
        in_specs=(
            P(EXP, None),
            P(),
            P(EXP, None, "dp"),
            P(EXP, None, "dp"),
            P(EXP, "dp", None),
            P(None, ALL),
            P(EXP, None),
            P(EXP),
        ),
        out_specs=(P(EXP, "dp"), P(ALL, None)),
        check_vma=False,
    )
```

```python
import functools

import jax
import jax.numpy as jnp
from jax import lax
from jax.experimental import pallas as pl
from jax.experimental.pallas import tpu as pltpu
from jax.sharding import Mesh, PartitionSpec as P

EXP = ("x", "y", "z")
ALL = ("x", "y", "z", "dp")
PLANE = ("x", "y")
F32 = jnp.float32
BF16 = jnp.bfloat16
LANES = 128
NT = (((1,), (1,)), ((), ()))
TN = (((0,), (0,)), ((), ()))


def dot(a, b):
    return jnp.dot(a, b, preferred_element_type=F32)


def dot_nt(a, b):
    return lax.dot_general(a, b, NT, preferred_element_type=F32)


def dot_tn(a, b):
    return lax.dot_general(a, b, TN, preferred_element_type=F32)


def split2(v):
    high = v.astype(BF16)
    return high, (v - high.astype(F32)).astype(BF16)


def half(start, size):
    return pl.ds(pl.multiple_of(start * size, LANES), size)


def slots_taken(ids_ref, shape):
    experts, rows, capacity = shape
    number = lax.broadcasted_iota(jnp.int32, (experts, rows), 0)
    hot0 = ids_ref[0:1, :] == number
    hot1 = ids_ref[1:2, :] == number
    member = jnp.where(hot0 | hot1, 1.0, 0.0)
    before = lax.broadcasted_iota(jnp.int32, (rows, rows), 0) < lax.broadcasted_iota(
        jnp.int32, (rows, rows), 1
    )
    earlier = dot(member.astype(BF16), jnp.where(before, 1.0, 0.0).astype(BF16))
    place = jnp.where(member > 0.0, earlier, -1.0)
    slots = lax.broadcasted_iota(jnp.int32, (experts, 2, capacity, rows), 2).astype(F32)
    return hot0, hot1, place[:, None, None, :] == slots


def prep_kernel(experts, capacity, d_ref, tok_hbm, ids_hbm, out_ref, tok_ref, ids_ref, sems):
    copies = [
        pltpu.make_async_copy(source, target, sems.at[k])
        for k, (source, target) in enumerate(((ids_hbm, ids_ref), (tok_hbm, tok_ref)))
    ]
    for copy in copies:
        copy.start()
    d = d_ref[0]
    rows, width = tok_ref.shape
    copies[0].wait()
    _, _, taken = slots_taken(ids_ref, (experts, rows, capacity))
    picks = jnp.where(taken, 1.0, 0.0).reshape(experts * 2 * capacity, rows).astype(BF16)
    copies[1].wait()
    out_ref[...] = dot(picks, tok_ref[:, half(d, width // 2)]).astype(BF16)


def gate_kernel(capacity, tok_ref, router_ref, ids_ref, high_ref, low_ref):
    rows = tok_ref.shape[0]
    experts = router_ref.shape[0]
    logits = dot_nt(router_ref[...], tok_ref[...])
    hot0, hot1, taken = slots_taken(ids_ref, (experts, rows, capacity))
    chosen0 = jnp.sum(jnp.where(hot0, logits, 0.0), axis=0, keepdims=True)
    chosen1 = jnp.sum(jnp.where(hot1, logits, 0.0), axis=0, keepdims=True)
    gate = jnp.where(hot0, jax.nn.sigmoid(chosen0 - chosen1), 0.0) + jnp.where(
        hot1, jax.nn.sigmoid(chosen1 - chosen0), 0.0
    )
    weights = jnp.where(taken, gate[:, None, None, :], 0.0).reshape(experts * 2 * capacity, rows)
    high_ref[...], low_ref[...] = split2(weights)


def order_kernel(*refs):
    pass


def load_kernel(gate_hbm, up_hbm, after_hbm, gate_ref, up_ref, sems):
    copies = [
        pltpu.make_async_copy(source, target, sems.at[k])
        for k, (source, target) in enumerate(((gate_hbm, gate_ref), (up_hbm, up_ref)))
    ]
    for copy in copies:
        copy.start()
    for copy in copies:
        copy.wait()


def ffn_kernel(
    step, block, d_ref, own_ref, other_ref, gate_ref, up_ref, down_hbm, hid_ref, out_ref, down_ref, sem
):
    d = d_ref[0]
    rows, part = own_ref.shape
    load_down = pltpu.make_async_copy(down_hbm, down_ref, sem)
    load_down.start()
    mine, theirs = half(d, part), half(1 - d, part)
    steps = [slice(m * step, (m + 1) * step) for m in range(rows // step)]
    for j in range(gate_ref.shape[1] // block):
        span = slice(j * block, (j + 1) * block)
        for at in steps:
            own, other = own_ref[at, :], other_ref[at, :]
            gate = dot(own, gate_ref[mine, span]) + dot(other, gate_ref[theirs, span])
            upper = dot(own, up_ref[mine, span]) + dot(other, up_ref[theirs, span])
            hid_ref[at, span] = (gate * jax.nn.sigmoid(gate) * upper).astype(BF16)
    load_down.wait()
    for at in steps:
        out_ref[at, :] = dot(hid_ref[at, :], down_ref[:, half(1 - d, part)]).astype(BF16)


def own_kernel(d_ref, hid_ref, down_ref, out_ref):
    out_ref[...] = dot(hid_ref[...], down_ref[:, half(d_ref[0], out_ref.shape[1])])


def add_kernel(own_ref, brought_ref, out_ref):
    out_ref[...] = (own_ref[...] + brought_ref[...].astype(F32)).astype(BF16)


def combine_kernel(d_ref, z_ref, back_ref, high_ref, low_ref, tok_ref, slot_ref, *refs):
    mixed_ref, payload_ref = refs[-2:]
    d, z = d_ref[0], z_ref[0]
    rows, part = mixed_ref.shape
    count = slot_ref.shape[0]
    back = back_ref[...]
    moe = dot_tn(high_ref[...], back) + dot_tn(low_ref[...], back)
    mixed = (tok_ref[:, half(d, part)].astype(F32) + moe).astype(BF16)
    mixed_ref[...] = mixed
    length = rows // count
    frames = jnp.sum(mixed.astype(F32).reshape(count, length, part), axis=1) / length
    slot = slot_ref[...]
    lane = lax.broadcasted_iota(jnp.int32, (count, part), 1)
    number = lax.broadcasted_iota(jnp.int32, (count, part), 0)
    digit = jnp.where(lane % (2 * count) < count, slot // 32, slot % 32)
    here = (lane // (2 * count) == z) & (lane % count == number)
    digits = jnp.sum(jnp.where(here, digit, 0).astype(F32), axis=0, keepdims=True)
    first = jnp.where(number == 0, jnp.broadcast_to(digits, (count, part)), 0.0)
    block = jnp.concatenate([frames, first], axis=0).astype(BF16)
    for k in range(payload_ref.shape[0]):
        payload_ref[k] = block


def clip_kernel(length, used, frames_ref, digits_ref, clips_ref):
    clips, part = clips_ref.shape
    groups = frames_ref.shape[0]
    digits = digits_ref[...].astype(F32)
    slot = digits[0:1, :] * 32.0 + digits[1:2, :]
    clip = jnp.floor(slot / length)
    number = lax.broadcasted_iota(jnp.int32, (clips, groups * used), 0).astype(F32)
    picks = jnp.where(clip == number, 1.0, 0.0).astype(BF16)
    frames = frames_ref[:, 0:used, :].reshape(groups * used, part)
    pooled = (dot(picks, frames) / length).astype(BF16)
    clips_ref[...] = pooled


def line_kernel(z_ref, clips_ref, *refs):
    line_refs, embed_ref = refs[:-1], refs[-1]
    pooled = clips_ref[...]
    count, chunk = len(line_refs), line_refs[0].shape[0]
    embed = dot_nt(jnp.concatenate([ref[...] for ref in line_refs], axis=0), pooled)
    for k in range(count):
        to = pl.ds(pl.multiple_of(lax.rem(z_ref[0] + count - k, count) * chunk, chunk), chunk)
        embed_ref[to, :] = embed[k * chunk : (k + 1) * chunk]


def cov_kernel(
    d_ref, x_ref, y_ref, own_ref, other_ref, cols_ref, cols_other_ref, plane0, plane1, plane2, plane3, out_ref
):
    d, x, y = d_ref[0], x_ref[0], y_ref[0]
    clips, part = own_ref.shape
    share = out_ref.shape[1]
    own, other = own_ref[...], other_ref[...]

    def center(embed):
        return embed - jnp.mean(embed, axis=1, keepdims=True)

    cols_high, cols_low = split2(center(cols_ref[...] + cols_other_ref[...]))
    planes = (plane0, plane1, plane2, plane3)
    mine = jnp.concatenate([ref[:, half(d, part)] for ref in planes], axis=0)
    theirs = jnp.concatenate([ref[:, half(1 - d, part)] for ref in planes], axis=0)
    rows_high, rows_low = split2(center(dot_nt(mine, own) + dot_nt(theirs, other)) / (clips - 1))
    block = dot_nt(rows_high, cols_high) + dot_nt(rows_high, cols_low) + dot_nt(rows_low, cols_high)
    block = block.astype(BF16)
    for j in range(4):
        for i in range(4):
            peer = 4 * lax.rem(x + 4 - i, 4) + lax.rem(y + 4 - j, 4)
            k = 4 * j + i
            out_ref[peer] = block[k * share : (k + 1) * share]


def place_kernel(in_ref, out_ref):
    peers, share, wide = in_ref.shape
    for k in range(peers):
        out_ref[:, k * wide : (k + 1) * wide] = in_ref[k].astype(F32)


SCALAR = pl.BlockSpec(memory_space=pltpu.SMEM)


def per_device(
    tokens,
    router_weight,
    gate_weight,
    up_weight,
    down_weight,
    expand_weight,
    expert_ids,
    frame_slot,
):
    tok_rows, width = tokens.shape
    experts = router_weight.shape[1]
    n_expert = lax.axis_size(EXP)
    n_z = lax.axis_size("z")
    n_xy = n_expert // n_z
    capacity = 4 * tok_rows // experts
    part = width // 2
    hidden = gate_weight.shape[2]
    rows = n_expert * capacity
    count = frame_slot.shape[0]
    frame_total = count * n_expert
    clip_total = frame_total // 4
    share = expand_weight.shape[1]
    d, x, y, z = (lax.axis_index(axis).astype(jnp.int32).reshape(1) for axis in ("dp", "x", "y", "z"))
    swap = [(0, 1), (1, 0)]
    params = pltpu.CompilerParams(vmem_limit_bytes=16 * 2**20)

    mine = expand_weight.T

    def ring(block, axis, step):
        size = lax.axis_size(axis)
        return lax.ppermute(block, axis, [(k, (k + step) % size) for k in range(size)])

    row = jnp.concatenate([mine] + [ring(mine, "x", step) for step in (1, 2, 3)], axis=0)
    planes = [row] + [ring(row, "y", step) for step in (1, 2, 3)]
    first, second = mine[:, :part], mine[:, part:]
    kept = jnp.where(d[0] == 0, first, second)
    sent = lax.ppermute(jnp.where(d[0] == 0, second, first), "dp", swap)
    both = jnp.concatenate(
        [jnp.where(d[0] == 0, kept, sent), jnp.where(d[0] == 0, sent, kept)], axis=0
    )
    along = {step: ring(both, "z", step) for step in (1, 7, 2, 6)}
    with_dispatch = (row, *(along[step] for step in (1, 7)), both)
    with_return = (*planes[1:], *(along[step] for step in (2, 6)))

    vmem = pl.BlockSpec(memory_space=pltpu.VMEM)
    hbm = pl.BlockSpec(memory_space=pl.ANY)
    outgoing = pl.pallas_call(
        functools.partial(prep_kernel, experts, capacity),
        out_shape=jax.ShapeDtypeStruct((rows, part), BF16),
        in_specs=[SCALAR, hbm, hbm],
        out_specs=vmem,
        scratch_shapes=[
            pltpu.VMEM(tokens.shape, BF16),
            pltpu.VMEM((2, tok_rows), jnp.int32),
            pltpu.SemaphoreType.DMA((2,)),
        ],
        compiler_params=pltpu.CompilerParams(vmem_limit_bytes=57 * 2**20),
        name="prep",
    )(d, tokens, expert_ids.T)
    high, low = pl.pallas_call(
        functools.partial(gate_kernel, capacity),
        out_shape=[jax.ShapeDtypeStruct((rows, tok_rows), BF16)] * 2,
        in_specs=[vmem] * 3,
        out_specs=(vmem, vmem),
        compiler_params=params,
        cost_estimate=pl.CostEstimate(
            flops=2 * tok_rows * width * experts, bytes_accessed=0, transcendentals=0
        ),
        name="gates",
    )(tokens, router_weight.T, expert_ids.T)

    received = lax.all_to_all(
        outgoing.reshape(n_expert, capacity, part), EXP, split_axis=0, concat_axis=0, tiled=True
    ).reshape(rows, part)
    with_dispatch = (high, low, *with_dispatch)
    received = pl.pallas_call(
        order_kernel,
        out_shape=jax.ShapeDtypeStruct((rows, part), BF16),
        in_specs=[hbm] * (1 + len(with_dispatch)),
        out_specs=hbm,
        input_output_aliases={0: 0},
        compiler_params=pltpu.CompilerParams(vmem_limit_bytes=2**20),
        name="order",
    )(received, *with_dispatch)
    other = lax.ppermute(received, "dp", swap)

    w_down = down_weight.reshape(hidden, width)
    w_gate, w_up = pl.pallas_call(
        load_kernel,
        out_shape=[jax.ShapeDtypeStruct((width, hidden), BF16)] * 2,
        in_specs=[hbm] * 3,
        out_specs=(vmem, vmem),
        scratch_shapes=[pltpu.SemaphoreType.DMA((2,))],
        compiler_params=pltpu.CompilerParams(vmem_limit_bytes=48 * 2**20),
        cost_estimate=pl.CostEstimate(flops=0, bytes_accessed=4 * width * hidden * 2, transcendentals=0),
        name="load",
    )(gate_weight.reshape(width, hidden), up_weight.reshape(width, hidden), received)
    inner, theirs = pl.pallas_call(
        functools.partial(ffn_kernel, 512, 256),
        out_shape=(
            jax.ShapeDtypeStruct((rows, hidden), BF16),
            jax.ShapeDtypeStruct((rows, part), BF16),
        ),
        in_specs=[SCALAR] + [vmem] * 4 + [hbm],
        out_specs=(vmem, vmem),
        scratch_shapes=[
            pltpu.VMEM((hidden, width), BF16),
            pltpu.SemaphoreType.DMA(()),
        ],
        compiler_params=pltpu.CompilerParams(vmem_limit_bytes=40 * 2**20),
        cost_estimate=pl.CostEstimate(
            flops=2 * rows * hidden * (2 * width + part), bytes_accessed=0, transcendentals=0
        ),
        name="ffn",
    )(d, received, other, w_gate, w_up, w_down)

    brought = lax.ppermute(theirs, "dp", swap)
    ours = pl.pallas_call(
        own_kernel,
        out_shape=jax.ShapeDtypeStruct((rows, part), F32),
        in_specs=[SCALAR, vmem, vmem],
        out_specs=vmem,
        compiler_params=params,
        cost_estimate=pl.CostEstimate(flops=2 * rows * hidden * part, bytes_accessed=0, transcendentals=0),
        name="ours",
    )(d, inner, w_down)
    summed = pl.pallas_call(
        add_kernel,
        out_shape=jax.ShapeDtypeStruct((rows, part), BF16),
        in_specs=[vmem, vmem],
        out_specs=vmem,
        compiler_params=params,
        name="total",
    )(ours, brought)
    back = lax.all_to_all(
        summed.reshape(n_expert, capacity, part), EXP, split_axis=0, concat_axis=0, tiled=True
    ).reshape(rows, part)

    mixed, payload = pl.pallas_call(
        combine_kernel,
        out_shape=(
            jax.ShapeDtypeStruct((tok_rows, part), BF16),
            jax.ShapeDtypeStruct((n_z, 2 * count, part), BF16),
        ),
        in_specs=[SCALAR] * 2 + [vmem] * 5 + [hbm] * len(with_return),
        out_specs=(vmem, vmem),
        compiler_params=params,
        name="combine",
    )(d, z, back, high, low, tokens, frame_slot.reshape(count, 1), *with_return)

    got = lax.all_to_all(payload, "z", split_axis=0, concat_axis=0, tiled=True)
    used = n_z * count
    wide = n_z * 2 * share
    packed = jnp.concatenate(
        [got[:, :count].reshape(used, part), jnp.sum(got[:, count:], axis=0)], axis=0
    )
    line = [both] + [along[step] if step in along else ring(both, "z", step) for step in range(1, n_z)]
    copies = jnp.broadcast_to(packed[None], (n_xy,) + packed.shape)
    gathered = lax.all_to_all(copies, PLANE, split_axis=0, concat_axis=0, tiled=True)
    digits = gathered[:, used, : 2 * used].reshape(n_xy, n_z, 2, count)
    digits = digits.transpose(2, 0, 1, 3).reshape(2, frame_total)
    clips = pl.pallas_call(
        functools.partial(clip_kernel, 4, used),
        out_shape=jax.ShapeDtypeStruct((clip_total, part), BF16),
        in_specs=[vmem, vmem],
        out_specs=vmem,
        compiler_params=params,
        name="clips",
    )(gathered, digits)
    other_clips = lax.ppermute(clips, "dp", swap)
    embed = pl.pallas_call(
        line_kernel,
        out_shape=jax.ShapeDtypeStruct((wide, clip_total), F32),
        in_specs=[SCALAR] + [vmem] * (1 + n_z),
        out_specs=vmem,
        compiler_params=params,
        cost_estimate=pl.CostEstimate(
            flops=2 * wide * part * clip_total, bytes_accessed=0, transcendentals=0
        ),
        name="line",
    )(z, clips, *line)
    other_embed = lax.ppermute(embed, "dp", swap)

    blocks = pl.pallas_call(
        cov_kernel,
        out_shape=jax.ShapeDtypeStruct((n_xy, share, wide), BF16),
        in_specs=[SCALAR] * 3 + [vmem] * 8,
        out_specs=vmem,
        compiler_params=params,
        name="covariance",
    )(d, x, y, clips, other_clips, embed, other_embed, *planes)
    home = lax.all_to_all(blocks, PLANE, split_axis=0, concat_axis=0, tiled=True)
    covariance = pl.pallas_call(
        place_kernel,
        out_shape=jax.ShapeDtypeStruct((share, n_xy * wide), F32),
        in_specs=[vmem],
        out_specs=vmem,
        compiler_params=params,
        name="place",
    )(home)
    return mixed, covariance


def solution(mesh):
    grid = Mesh(mesh.devices.reshape(4, 4, 8, 2), ALL)
    return jax.shard_map(
        per_device,
        mesh=grid,
        in_specs=(
            P(EXP, None),
            P(),
            P(EXP, None, "dp"),
            P(EXP, None, "dp"),
            P(EXP, "dp", None),
            P(None, ALL),
            P(EXP, None),
            P(EXP),
        ),
        out_specs=(P(EXP, "dp"), P(ALL, None)),
        check_vma=False,
    )
```
